256 devices in a mesh: grp: 8 (over y, x_lo), sp: 32 (over x_hi, z, core).
Axes of the slice: x: 4 (x_hi: 2, x_lo: 2; x = x_hi * 2 + x_lo), y: 4, z: 8, core: 2. Of those that a mesh axis runs over, the one named last changes fastest.
Arguments:
- fields: bfloat16 [8, 128, 16, 16, 192], P('grp', 'sp'), may hold values from -6 to 6
- depth_kernel: float32 [7, 7, 192], replicated, may hold values from -0.875 to 0.875
- layer_norm_gain: float32 [192], replicated, may hold values from 0.1 to 1.9
- layer_norm_bias: float32 [192], replicated, may hold values from -3 to 3
- up_weight: bfloat16 [192, 768], replicated, may hold values from -0.4375 to 0.4375
- up_bias: float32 [768], replicated, may hold values from -3 to 3
- down_weight: bfloat16 [768, 192], replicated, may hold values from -0.21875 to 0.21875
- cotangent: bfloat16 [8, 128, 16, 16, 192], P('grp', 'sp'), may hold values from -6 to 6
- neighbours: int32 [128, 8], replicated, may hold values from 0 to 127, as said below
- rotation: int32 [128, 8], replicated, may hold values from 0 to 3, as said below
- tile_owner: int32 [128], replicated, may hold values from 0 to 127, as said below
Outputs:
- updated: bfloat16 [8, 128, 16, 16, 192], P('grp', 'sp')
- grad_fields: bfloat16 [8, 128, 16, 16, 192], P('grp', 'sp')
- grad_kernel: float32 [7, 7, 192], replicated
- grad_gain: float32 [192], replicated
- grad_bias: float32 [192], replicated
- grad_up_weight: float32 [192, 768], replicated
- grad_up_bias: float32 [768], replicated
- grad_down_weight: float32 [768, 192], replicated
The draws below stay inside these ranges and needn't reach their ends.
Inputs may be any that keep to these rules, and one draw needn't show every extreme that they name: neighbours[q, s] is the tile beside tile q in slot s, and the relation is mutual (top with bottom, left with right, each corner with the opposite one). For the tile in storage row p, every neighbour's storage row lies in block p // 4 - 1, p // 4 or p // 4 + 1 (blocks of 4 rows, counted cyclically over 32 blocks). `rotation`: quarter turns counterclockwise applied to the neighbour tile before its border is read; the turn that tile q gives its neighbour and the turn that the neighbour gives q add up to a multiple of 4. `tile_owner`: a permutation of the storage rows.
All inputs are finite; a program needn't handle non-finite values.
Results may differ from the reference program's by a relative error of at most 0.0056.
Values may be sent and summed in bfloat16 or wider, within the bound.
No kernel may reach another device: no remote copies, remote signals or barrier semaphores. Data moves between devices by JAX's collectives and lax.ppermute only.
A program may use at most 128 MiB of HBM per device.

```python
import math
import jax
import jax.numpy as jnp
from jax import lax

C = 192
HID = 768
TPD = 4
S = 16
GROUPS = 8
TILES = 128


def tile_layout(key):
    grid_rows = TILES // TPD
    subkeys = jax.random.split(key, 4)
    row_twist = jax.random.randint(subkeys[0], (grid_rows,), 0, TPD)
    tile_label = jax.random.permutation(subkeys[1], TILES).astype(jnp.int32)
    placing = jax.vmap(lambda subkey: jax.random.permutation(subkey, TPD))(jax.random.split(subkeys[2], grid_rows)).astype(jnp.int32)
    row_turn = jax.random.randint(subkeys[3], (grid_rows,), 0, 4)
    every_row = jnp.arange(grid_rows, dtype=jnp.int32)
    polar_row = (every_row < grid_rows // 4) | (every_row >= grid_rows - grid_rows // 4)
    row_turn = row_turn * polar_row.astype(jnp.int32)
    cell_index = jnp.arange(TILES, dtype=jnp.int32)
    row_index = cell_index // TPD
    column = cell_index % TPD
    upper_row = (row_index - 1) % grid_rows
    lower_row = (row_index + 1) % grid_rows
    bend_here = row_twist[row_index]
    bend_below = row_twist[lower_row]

    def cell_at(which_row, which_column):
        return which_row * TPD + which_column % TPD
    near_cells = jnp.stack([cell_at(upper_row, column + bend_here), cell_at(lower_row, column - bend_below), cell_at(row_index, column - 1), cell_at(row_index, column + 1), cell_at(upper_row, column - 1 + bend_here), cell_at(upper_row, column + 1 + bend_here), cell_at(lower_row, column - 1 - bend_below), cell_at(lower_row, column + 1 - bend_below)], axis=1)
    quarter_turns = (row_turn[near_cells // TPD] - row_turn[row_index][:, None]) % 4
    neighbour_ids = jnp.zeros((TILES, 8), jnp.int32).at[tile_label].set(tile_label[near_cells])
    rotation_codes = jnp.zeros((TILES, 8), jnp.int32).at[tile_label].set(quarter_turns.astype(jnp.int32))
    owner_rows = jnp.zeros((TILES,), jnp.int32).at[tile_label].set(row_index * TPD + placing[row_index, column])
    return (neighbour_ids, rotation_codes, owner_rows)


def draw_neighbours(key, part):
    shared = tile_layout(key)
    return shared[0]


def draw_rotation(key, part):
    shared = tile_layout(key)
    return shared[1]


def draw_tile_owner(key, part):
    shared = tile_layout(key)
    return shared[2]


def levels(key, extent, pieces, low, high):
    factor_of = 1.0
    for dim, blocks in pieces:
        heights = jax.random.uniform(jax.random.fold_in(jax.random.fold_in(key, 6), dim), (blocks,), jnp.float32, low / len(pieces), high / len(pieces))
        factor_of = factor_of * jnp.repeat(jnp.exp(heights), extent[dim] // blocks).reshape((-1,) + (1,) * (len(extent) - 1 - dim))
    return factor_of


def scatter_about(own_key, shape, width, reach, pieces=(), kind=jnp.bfloat16):
    gain = levels(own_key, shape, pieces, -0.22, 0.18) if pieces else 1.0
    drawn = jax.random.normal(own_key, shape, jnp.float32) * width * gain
    return jnp.minimum(jnp.maximum(drawn, -reach), reach).astype(kind)


def setup_inputs(seed: int = 0) -> dict:
    key_list = jax.random.split(jax.random.key(seed), 12)
    return {
        "fields": scatter_about(key_list[0], (GROUPS, TILES, S, S, C), 1.0, 6.0, ((0, 8), (1, 32))),
        "depth_kernel": scatter_about(key_list[1], (7, 7, C), 49 ** -0.5, 0.875, (), jnp.float32),
        "layer_norm_gain": jnp.clip(1.0 + 0.18 * jax.random.normal(key_list[2], (C,), jnp.float32), 0.1, 1.9),
        "layer_norm_bias": scatter_about(key_list[3], (C,), 0.5, 3.0, (), jnp.float32),
        "up_weight": scatter_about(key_list[4], (C, HID), C ** -0.5, 0.4375),
        "up_bias": scatter_about(key_list[5], (HID,), 0.5, 3.0, (), jnp.float32),
        "down_weight": scatter_about(key_list[6], (HID, C), HID ** -0.5, 0.21875),
        "cotangent": scatter_about(key_list[7], (GROUPS, TILES, S, S, C), 1.0, 6.0, ((0, 8), (1, 32))),
        "neighbours": draw_neighbours(jax.random.fold_in(key_list[11], 71), 0),
        "rotation": draw_rotation(jax.random.fold_in(key_list[11], 71), 0),
        "tile_owner": draw_tile_owner(jax.random.fold_in(key_list[11], 71), 0),
    }


GELU_C = math.sqrt(2.0 / math.pi)
EPSILON = 1e-06

def gelu_pair(value):
    cubic = 0.044715 * value * value * value
    tangent = jnp.tanh(GELU_C * (value + cubic))
    result = 0.5 * value * (1.0 + tangent)
    slope = 0.5 * (1.0 + tangent) + 0.5 * value * (1.0 - tangent * tangent) * GELU_C * (1.0 + 3.0 * 0.044715 * value * value)
    return (result, slope)

def turned(tiles, quarter_turns):
    result = tiles
    for quarter in range(1, 4):
        result = jnp.where((quarter_turns == quarter)[:, None, None, None], jnp.rot90(tiles, quarter, axes=(1, 2)), result)
    return result

def padded_tiles(sample, near_rows, quarter_turns):

    def slot_tile(slot_number):
        return turned(sample[near_rows[:, slot_number]], quarter_turns[:, slot_number])
    top_band = slot_tile(0)[:, S - 3:, :, :]
    bottom_band = slot_tile(1)[:, :3, :, :]
    left_band = slot_tile(2)[:, :, S - 3:, :]
    right_band = slot_tile(3)[:, :, :3, :]
    top_left = slot_tile(4)[:, S - 3:, S - 3:, :]
    top_right = slot_tile(5)[:, S - 3:, :3, :]
    bottom_left = slot_tile(6)[:, :3, S - 3:, :]
    bottom_right = slot_tile(7)[:, :3, :3, :]
    upper = jnp.concatenate([top_left, top_band, top_right], axis=2)
    middle = jnp.concatenate([left_band, sample, right_band], axis=2)
    lower = jnp.concatenate([bottom_left, bottom_band, bottom_right], axis=2)
    return jnp.concatenate([upper, middle, lower], axis=1)

def reference(fields, depth_kernel, layer_norm_gain, layer_norm_bias, up_weight, up_bias, down_weight, cotangent, neighbours, rotation, tile_owner):
    tile_id = jnp.zeros((TILES,), jnp.int32).at[tile_owner].set(jnp.arange(TILES, dtype=jnp.int32))
    near_rows = tile_owner[neighbours[tile_id]]
    quarter_turns = rotation[tile_id]
    scale = 1.0 / math.sqrt(GROUPS * TILES * S * S)

    def one_sample(carry, pair):
        sample, cotan = pair
        padded = padded_tiles(sample, near_rows, quarter_turns)
        mixed = jnp.zeros((TILES, S, S, C), jnp.float32)
        for offset_row in range(7):
            for offset_col in range(7):
                mixed = mixed + padded[:, offset_row:offset_row + S, offset_col:offset_col + S, :].astype(jnp.float32) * depth_kernel[offset_row, offset_col]
        average = lax.optimization_barrier(jnp.mean(mixed, axis=-1, keepdims=True))
        mean_removed = mixed - average
        variance = lax.optimization_barrier(jnp.mean(mean_removed * mean_removed, axis=-1, keepdims=True))
        inverse_deviation = lax.rsqrt(variance + EPSILON)
        standardized_input = mean_removed * inverse_deviation
        normalized_output = (standardized_input * layer_norm_gain + layer_norm_bias).astype(jnp.bfloat16)
        flat_normed = normalized_output.reshape(-1, C)
        up_value = jnp.dot(flat_normed, up_weight, preferred_element_type=jnp.float32) + up_bias
        gelu_value, gelu_slope = gelu_pair(up_value)
        activation = gelu_value.astype(jnp.bfloat16)
        branch = jnp.dot(activation, down_weight, preferred_element_type=jnp.float32).reshape(TILES, S, S, C)
        updated = (sample.astype(jnp.float32) + branch).astype(jnp.bfloat16)
        flat_cotan = cotan.reshape(-1, C)
        d_up = jnp.dot(flat_cotan, down_weight.T, preferred_element_type=jnp.float32) * gelu_slope
        d_up_b = d_up.astype(jnp.bfloat16)
        grad_down = jnp.dot(activation.T, flat_cotan, preferred_element_type=jnp.float32)
        grad_up = jnp.dot(flat_normed.T, d_up_b, preferred_element_type=jnp.float32)
        grad_up_b = lax.optimization_barrier(jnp.sum(d_up, axis=0))
        normalized_gradient = jnp.dot(d_up_b, up_weight.T, preferred_element_type=jnp.float32).reshape(TILES, S, S, C)
        gain_gradient = lax.optimization_barrier(jnp.sum(normalized_gradient * standardized_input, axis=(0, 1, 2)))
        grad_b = lax.optimization_barrier(jnp.sum(normalized_gradient, axis=(0, 1, 2)))
        gain_scaled = normalized_gradient * layer_norm_gain
        mixed_gradient = inverse_deviation * (gain_scaled - lax.optimization_barrier(jnp.mean(gain_scaled, axis=-1, keepdims=True)) - standardized_input * lax.optimization_barrier(jnp.mean(gain_scaled * standardized_input, axis=-1, keepdims=True)))
        spread = jnp.pad(mixed_gradient, ((0, 0), (6, 6), (6, 6), (0, 0)))
        d_padded = jnp.zeros((TILES, S + 6, S + 6, C), jnp.float32)
        kernel_terms = []
        for offset_row in range(7):
            for offset_col in range(7):
                d_padded = d_padded + depth_kernel[offset_row, offset_col] * spread[:, 6 - offset_row:12 + S - offset_row, 6 - offset_col:12 + S - offset_col, :]
                kernel_terms.append(lax.optimization_barrier(jnp.sum(padded[:, offset_row:offset_row + S, offset_col:offset_col + S, :].astype(jnp.float32) * mixed_gradient, axis=(0, 1, 2))))
        grad_k = jnp.stack(kernel_terms).reshape(7, 7, C)
        _, pull_back = jax.vjp(lambda values: padded_tiles(values, near_rows, quarter_turns), sample.astype(jnp.float32))
        d_sample = pull_back(d_padded)[0]
        grad_x = (cotan.astype(jnp.float32) + d_sample).astype(jnp.bfloat16)
        terms = (grad_k, gain_gradient, grad_b, grad_up, grad_up_b, grad_down)
        carry = tuple((held + term for held, term in zip(carry, terms)))
        return (carry, (updated, grad_x))
    start = (jnp.zeros((7, 7, C), jnp.float32), jnp.zeros((C,), jnp.float32), jnp.zeros((C,), jnp.float32), jnp.zeros((C, HID), jnp.float32), jnp.zeros((HID,), jnp.float32), jnp.zeros((HID, C), jnp.float32))
    sums, stacked = lax.scan(one_sample, start, (fields, cotangent))
    updated, grad_fields = stacked
    return (updated, grad_fields, sums[0] * scale, sums[1] * scale, sums[2] * scale, sums[3] * scale, sums[4] * scale, sums[5] * scale)
```

```python
import math

import jax
import jax.numpy as jnp
from jax import lax
from jax.experimental import pallas as pl
from jax.experimental.pallas import tpu as pltpu
from jax.sharding import Mesh, PartitionSpec as P

GELU_C = math.sqrt(2.0 / math.pi)
EPSILON = 1e-06
F32 = jnp.float32
BF16 = jnp.bfloat16
T = 4
S = 16
PX = S * S
C = 192
HID = 768
W = 24
DW = 32
WEIGHT_ROWS = 2 * C * HID // 128
ROWS = 2560


def gelu_pair(value):
    square = value * value
    tangent = jnp.tanh(GELU_C * (value + 0.044715 * square * value))
    half = 0.5 * (1.0 + tangent)
    result = value * half
    slope = half + 0.5 * value * (1.0 - tangent * tangent) * (GELU_C + GELU_C * 3.0 * 0.044715 * square)
    return (result, slope)


def turn_of(quarter):
    on_i = jnp.where(quarter == 0, S, jnp.where(quarter == 1, -1, jnp.where(quarter == 2, -S, 1)))
    on_j = jnp.where(quarter == 0, 1, jnp.where(quarter == 1, S, jnp.where(quarter == 2, -1, -S)))
    base = jnp.where(
        quarter == 0, 0, jnp.where(quarter == 1, S - 1, jnp.where(quarter == 2, PX - 1, PX - S))
    )
    return on_i, on_j, base


SLOTS = (
    (0, S - 3, -3, 3, 19),
    (2, 0, -3, 3, 19),
    (1, 0, S - 3, 0, 3),
    (1, 0, -19, 19, 22),
    (0, S - 3, S - 3, 0, 3),
    (0, S - 3, -19, 19, 22),
    (2, 0, S - 3, 0, 3),
    (2, 0, -19, 19, 22),
)
FIRST = (0, 3, 19)
COUNT = (3, S, 3)


def slot_match(slot, quarter, transposed):
    group, row0, col0, low, high = SLOTS[slot]
    length = COUNT[group] * W
    shape = (PX, length) if transposed else (length, PX)
    along = 1 if transposed else 0
    line = (1, length) if transposed else (length, 1)
    place = lax.broadcasted_iota(jnp.int32, line, along)
    row = place // W
    col = place - row * W
    on_i, on_j, base = turn_of(quarter)
    source = on_i * (row + row0) + on_j * (col + col0) + base
    source = jnp.where((col >= low) & (col < high), source, -1)
    return (lax.broadcasted_iota(jnp.int32, shape, 1 - along) == source).astype(F32).astype(BF16)


def block_kernel(
    pos_ref,
    turn_ref,
    prev_ref,
    own_ref,
    next_ref,
    cot_ref,
    cot_t_ref,
    kern_ref,
    gain_ref,
    bias_ref,
    up_ref,
    up_bias_ref,
    down_t_ref,
    down_ref,
    up_t_ref,
    updated_ref,
    part_ref,
    to_prev_ref,
    to_next_ref,
    grads_ref,
    src,
    pad,
    mix,
    xhat,
    inv,
    normed,
    dmix,
    dpad,
    collected,
    g_up,
    g_down_t,
    g_up_bias,
    g_small,
):
    lane = lax.broadcasted_iota(jnp.int32, (1, 128), 1)
    low_half = lane < 64

    src[:, :, 128:] = jnp.zeros((3 * T, PX, 128), BF16)
    src[0:T, :, :C] = prev_ref[...]
    src[T : 2 * T, :, :C] = own_ref[...]
    src[2 * T :, :, :C] = next_ref[...]
    g_up[...] = jnp.zeros_like(g_up)
    g_down_t[...] = jnp.zeros_like(g_down_t)
    g_up_bias[...] = jnp.zeros_like(g_up_bias)
    g_small[...] = jnp.zeros_like(g_small)
    dmix[...] = jnp.zeros_like(dmix)
    collected[...] = jnp.zeros_like(collected)

    @pl.loop(0, T // 2)
    def _(pair):
        for half in range(2):
            tile = pair * 2 + half
            for group in range(3):
                total = None
                for slot in range(8):
                    if SLOTS[slot][0] != group:
                        continue
                    match = slot_match(slot, turn_ref[tile * 8 + slot], False)
                    piece = jnp.dot(
                        match, src[pos_ref[tile * 8 + slot]], preferred_element_type=F32
                    )
                    total = piece if total is None else total + piece
                if group == 1:
                    place = lax.broadcasted_iota(jnp.int32, (S * W, 1), 0)
                    row = place // W
                    col = place - row * W - 3
                    source = jnp.where((col >= 0) & (col < S), row * S + col, -1)
                    match = lax.broadcasted_iota(jnp.int32, (S * W, PX), 1) == source
                    total = total + jnp.dot(
                        match.astype(F32).astype(BF16), src[T + tile], preferred_element_type=F32
                    )
                rows = pl.ds(FIRST[group] * W, COUNT[group] * W)
                if half == 0:
                    pad[pair * 3, rows, :] = total[:, :128]
                    pad[pair * 3 + 1, rows, :] = total[:, 128:]
                else:
                    total = pltpu.roll(total, 64, 1)
                    pad[pair * 3 + 1, rows, :] += total[:, :128]
                    pad[pair * 3 + 2, rows, :] = total[:, 128:]

    @pl.loop(0, 3 * T // 2)
    def _(slab):
        part = lax.rem(slab, 3)
        for half in range(2):
            acc = [None] * S
            for b in range(7):
                taps = [kern_ref[part, a * 7 + b : a * 7 + b + 1, :] for a in range(7)]
                for m in range(S + 6):
                    x = pad[slab, pl.ds(m * W + b + 8 * half, 8), :]
                    for a in range(7):
                        i = m - a
                        if 0 <= i < S:
                            term = x * taps[a]
                            acc[i] = term if acc[i] is None else acc[i] + term
            for i in range(S):
                mix[slab, pl.ds(i * S + 8 * half, 8), :] = acc[i]

    def pair_means(s0, s1, s2):
        first = jnp.sum(s0 + jnp.where(low_half, s1, 0.0), axis=1, keepdims=True) * (1.0 / C)
        second = jnp.sum(s2 + jnp.where(low_half, 0.0, s1), axis=1, keepdims=True) * (1.0 / C)
        return first, jnp.where(low_half, first, second), second

    CH = 64

    @pl.loop(0, (T // 2) * (PX // CH))
    def _(step):
        pair = step // (PX // CH)
        rows = pl.ds(pl.multiple_of(lax.rem(step, PX // CH) * CH, CH), CH)
        slabs = [mix[pair * 3 + k, rows, :] for k in range(3)]
        means = pair_means(*slabs)
        slabs = [x - m for x, m in zip(slabs, means)]
        spreads = pair_means(*[x * x for x in slabs])
        for k in range(3):
            deviation = jnp.broadcast_to(lax.rsqrt(spreads[k] + EPSILON), (CH, 128))
            standard = slabs[k] * deviation
            inv[pair * 3 + k, rows, :] = deviation
            xhat[pair * 3 + k, rows, :] = standard
            normed[pair, rows, 128 * k : 128 * (k + 1)] = (
                standard * gain_ref[k] + bias_ref[k]
            ).astype(BF16)

    @pl.loop(0, T // 2)
    def _(pair):
        normed_grads = []
        for half in range(2):
            tile = pair * 2 + half
            x = normed[pair, :, 128 * half : 128 * half + 256]
            x_t = jnp.transpose(x.astype(F32)).astype(BF16)
            cot = cot_ref[tile]
            cot_t = cot_t_ref[tile]
            branch = jnp.zeros((PX, C), F32)
            normed_grad = jnp.zeros((PX, 256), F32)
            for chunk in range(3):
                hid = slice(256 * chunk, 256 * (chunk + 1))
                up_value = (
                    jnp.dot(x, up_ref[half, :, hid], preferred_element_type=F32)
                    + up_bias_ref[:, hid]
                )
                value, slope = gelu_pair(up_value)
                activation = value.astype(BF16)
                branch += jnp.dot(activation, down_ref[hid, :], preferred_element_type=F32)
                d_up = jnp.dot(cot, down_t_ref[:, hid], preferred_element_type=F32) * slope
                g_up_bias[:, hid] += jnp.sum(d_up.reshape(PX // 8, 8, 256), axis=0)
                d_up_b = d_up.astype(BF16)
                g_down_t[:, hid] += jnp.dot(cot_t, activation, preferred_element_type=F32)
                up_grad = jnp.dot(x_t, d_up_b, preferred_element_type=F32)
                g_up[:, hid] += up_grad[64 * half : 64 * half + C]
                normed_grad += jnp.dot(d_up_b, up_t_ref[half, hid, :], preferred_element_type=F32)
            updated_ref[tile] = (own_ref[tile].astype(F32) + branch).astype(BF16)
            normed_grads.append(normed_grad)
        mix[pair * 3] = normed_grads[0][:, :128]
        mix[pair * 3 + 1] = normed_grads[0][:, 128:] + normed_grads[1][:, :128]
        mix[pair * 3 + 2] = normed_grads[1][:, 128:]

    @pl.loop(0, (T // 2) * (PX // CH))
    def _(step):
        pair = step // (PX // CH)
        start = pl.multiple_of(lax.rem(step, PX // CH) * CH, CH)
        rows = pl.ds(start, CH)
        grads = [mix[pair * 3 + k, rows, :] for k in range(3)]
        standard = [xhat[pair * 3 + k, rows, :] for k in range(3)]
        for k in range(3):
            g_small[k, 8 * 49 : 8 * 50, :] += jnp.sum(
                (grads[k] * standard[k]).reshape(CH // 8, 8, 128), axis=0
            )
            g_small[k, 8 * 50 : 8 * 51, :] += jnp.sum(grads[k].reshape(CH // 8, 8, 128), axis=0)
        scaled = [grads[k] * gain_ref[k] for k in range(3)]
        means = pair_means(*scaled)
        products = pair_means(*[e * x for e, x in zip(scaled, standard)])
        for k in range(3):
            d_mixed = inv[pair * 3 + k, rows, :] * (
                scaled[k] - means[k] - standard[k] * products[k]
            )
            for r in range(CH // S):
                at = (start // S + r) * DW + 8
                dmix[pair * 3 + k, pl.ds(pl.multiple_of(at, 8), S), :] = d_mixed[r * S : (r + 1) * S]

    @pl.loop(0, 3 * T // 2)
    def _(slab):
        part = lax.rem(slab, 3)
        for half in range(2):
            grads = [dmix[slab, pl.ds(i * DW + 8 + 8 * half, 8), :] for i in range(S)]
            for b in range(7):
                acc = [None] * 7
                for m in range(S + 6):
                    x = pad[slab, pl.ds(m * W + b + 8 * half, 8), :]
                    for a in range(7):
                        i = m - a
                        if 0 <= i < S:
                            term = x * grads[i]
                            acc[a] = term if acc[a] is None else acc[a] + term
                for a in range(7):
                    g_small[part, 8 * (a * 7 + b) : 8 * (a * 7 + b + 1), :] += acc[a]
        for third in range(3):
            acc = [None] * (S + 6)
            for b in range(7):
                taps = [kern_ref[part, a * 7 + b : a * 7 + b + 1, :] for a in range(7)]
                for i in range(S):
                    x = dmix[slab, pl.ds(i * DW + 8 + 8 * third - b, 8), :]
                    for a in range(7):
                        term = x * taps[a]
                        acc[i + a] = term if acc[i + a] is None else acc[i + a] + term
            for m in range(S + 6):
                dpad[slab, pl.ds(m * W + 8 * third, 8), :] = acc[m]

    @pl.loop(0, T // 2)
    def _(pair):
        for half in range(2):
            tile = pair * 2 + half
            for slot in range(8):
                group = SLOTS[slot][0]
                rows = pl.ds(FIRST[group] * W, COUNT[group] * W)
                border = jnp.concatenate(
                    [dpad[pair * 3 + half + k, rows, :] for k in range(2)], axis=1
                ).astype(BF16)
                match = slot_match(slot, turn_ref[tile * 8 + slot], True)
                piece = jnp.dot(match, border, preferred_element_type=F32)
                if half == 1:
                    piece = pltpu.roll(piece, 192, 1)
                collected[pos_ref[tile * 8 + slot]] += piece

    to_prev_ref[...] = collected[0:T, :, :C].astype(BF16)
    to_next_ref[...] = collected[2 * T :, :, :C].astype(BF16)

    @pl.loop(0, T // 2)
    def _(pair):
        for half in range(2):
            tile = pair * 2 + half
            for i in range(S):
                rows = slice(i * S, (i + 1) * S)
                centre = jnp.concatenate(
                    [dpad[pair * 3 + half + k, pl.ds((i + 3) * W + 3, S), :] for k in range(2)],
                    axis=1,
                )
                if half == 1:
                    centre = pltpu.roll(centre, 192, 1)
                part_ref[tile, rows, :] = (
                    cot_ref[tile, rows, :].astype(F32)
                    + centre[:, :C]
                    + collected[T + tile, rows, :C]
                )

    for k in range(HID // 128):
        lanes = slice(128 * k, 128 * (k + 1))
        grads_ref[C * k : C * (k + 1), :] = g_up[:, lanes].astype(BF16)
        grads_ref[WEIGHT_ROWS // 2 + C * k : WEIGHT_ROWS // 2 + C * (k + 1), :] = g_down_t[
            :, lanes
        ].astype(BF16)
    sums = [jnp.sum(g_small[k].reshape(56, 8, 128), axis=1) for k in range(3)]
    crossed = pltpu.roll(jnp.where(low_half, sums[2], sums[1]), 64, 1)
    grads_ref[WEIGHT_ROWS : WEIGHT_ROWS + 56, :] = (sums[0] + crossed).astype(BF16)
    grads_ref[WEIGHT_ROWS + 56 : WEIGHT_ROWS + 112, :] = (
        sums[1] + pltpu.roll(sums[2], 64, 1)
    ).astype(BF16)
    bias_sum = jnp.sum(g_up_bias[...], axis=0, keepdims=True)
    bias_rows = jnp.concatenate(
        [bias_sum[:, 128 * k : 128 * (k + 1)] for k in range(6)] + [jnp.zeros((10, 128), F32)],
        axis=0,
    )
    grads_ref[WEIGHT_ROWS + 112 : WEIGHT_ROWS + 128, :] = bias_rows.astype(BF16)
    grads_ref[WEIGHT_ROWS + 128 :, :] = jnp.zeros((ROWS - WEIGHT_ROWS - 128, 128), BF16)


def run_block(pos, turns, prev, own, nxt, cot, cot_t, kern, gain, bias, up, up_bias, down_t, down, up_t):
    vmem = pl.BlockSpec(memory_space=pltpu.VMEM)
    smem = pl.BlockSpec(memory_space=pltpu.SMEM)
    slabs = 3 * T // 2
    tile = (T, PX, C)
    return pl.pallas_call(
        block_kernel,
        out_shape=(
            jax.ShapeDtypeStruct(tile, BF16),
            jax.ShapeDtypeStruct(tile, F32),
            jax.ShapeDtypeStruct(tile, BF16),
            jax.ShapeDtypeStruct(tile, BF16),
            jax.ShapeDtypeStruct((ROWS, 128), BF16),
        ),
        in_specs=[smem, smem] + [vmem] * 13,
        out_specs=(vmem,) * 5,
        scratch_shapes=[
            pltpu.VMEM((3 * T, PX, 256), BF16),
            pltpu.VMEM((slabs, 22 * W, 128), F32),
            pltpu.VMEM((slabs, PX, 128), F32),
            pltpu.VMEM((slabs, PX, 128), F32),
            pltpu.VMEM((slabs, PX, 128), F32),
            pltpu.VMEM((T // 2, PX, 384), BF16),
            pltpu.VMEM((slabs, S * DW, 128), F32),
            pltpu.VMEM((slabs, 22 * W, 128), F32),
            pltpu.VMEM((3 * T, PX, 256), F32),
            pltpu.VMEM((C, HID), F32),
            pltpu.VMEM((C, HID), F32),
            pltpu.VMEM((8, HID), F32),
            pltpu.VMEM((3, 8 * 56, 128), F32),
        ],
        compiler_params=pltpu.CompilerParams(vmem_limit_bytes=48 * 1024 * 1024),
        cost_estimate=pl.CostEstimate(flops=4 * 10**9, bytes_accessed=8 * 10**6, transcendentals=10**6),
    )(pos, turns, prev, own, nxt, cot, cot_t, kern, gain, bias, up, up_bias, down_t, down, up_t)


FLAT = ("y", "xl", "xh", "z")


def shared_with(x, axes, count):
    return lax.all_to_all(jnp.broadcast_to(x[None], (count,) + x.shape), axes, 0, 0)


def total_of(x):
    return jnp.sum(x.astype(F32), axis=0)


def sum_everywhere(grads):
    core = lax.axis_index("c")
    swap = [(0, 1), (1, 0)]
    halves = grads.reshape(2, ROWS // 2, 128)
    other = lax.ppermute(lax.dynamic_index_in_dim(halves, 1 - core, 0, keepdims=False), "c", swap)
    mine = lax.dynamic_index_in_dim(halves, core, 0, keepdims=False)
    mine = (mine.astype(F32) + other.astype(F32)).astype(BF16)
    plane = ("y", "xl", "xh")
    mine = total_of(lax.all_to_all(mine.reshape(16, ROWS // 32, 128), plane, 0, 0))
    mine = total_of(shared_with(mine.astype(BF16), "z", 8))
    mine = shared_with(mine.astype(BF16), plane, 16).reshape(ROWS // 2, 128)
    other = lax.ppermute(mine, "c", swap)
    return jnp.concatenate([jnp.where(core == 0, mine, other), jnp.where(core == 0, other, mine)])


def on_device(
    fields,
    depth_kernel,
    layer_norm_gain,
    layer_norm_bias,
    up_weight,
    up_bias,
    down_weight,
    cotangent,
    neighbours,
    rotation,
    tile_owner,
):
    around = ("xh", "z", "c")
    blocks = 32
    position = lax.axis_index(around)
    to_right = [(i, (i + 1) % blocks) for i in range(blocks)]
    to_left = [((i + 1) % blocks, i) for i in range(blocks)]
    own = fields.reshape(T, PX, C)
    cot = cotangent.reshape(T, PX, C)
    prev = lax.ppermute(own, around, to_right)
    nxt = lax.ppermute(own, around, to_left)

    every = jnp.arange(128, dtype=jnp.int32)
    own_rows = position * T + jnp.arange(T, dtype=jnp.int32)
    is_own = (tile_owner[None, :] == own_rows[:, None]).astype(jnp.int32)
    near_ids = jnp.sum(is_own[:, :, None] * neighbours[None], axis=1)
    turns = jnp.sum(is_own[:, :, None] * rotation[None], axis=1)
    near_rows = jnp.sum((near_ids[:, :, None] == every) * tile_owner, axis=2)
    pos = (near_rows // T - position + 1) % blocks * T + near_rows % T

    def packed(x):
        return jnp.concatenate([x, x], axis=-1).reshape(x.shape[:-1] + (3, 128))

    kern = jnp.transpose(packed(depth_kernel.reshape(49, C)), (1, 0, 2))
    kern = jnp.pad(kern, ((0, 0), (0, 7), (0, 0)))
    gain = packed(layer_norm_gain)[:, None, :]
    bias = packed(layer_norm_bias)[:, None, :]
    up = jnp.stack(
        [jnp.pad(up_weight, ((0, 64), (0, 0))), jnp.pad(up_weight, ((64, 0), (0, 0)))]
    )
    up_t = jnp.transpose(up, (0, 2, 1))
    updated, part, to_prev, to_next, grads = run_block(
        pos.reshape(-1),
        turns.reshape(-1),
        prev,
        own,
        nxt,
        cot,
        jnp.transpose(cot, (0, 2, 1)),
        kern,
        gain,
        bias,
        up,
        up_bias[None],
        down_weight.T,
        down_weight,
        up_t,
    )
    from_right = lax.ppermute(to_prev, around, to_left)
    from_left = lax.ppermute(to_next, around, to_right)
    sums = sum_everywhere(grads)
    grad_fields = (part + from_right.astype(F32) + from_left.astype(F32)).astype(BF16)

    scale = 1.0 / math.sqrt(8 * blocks * T * PX)
    sums = sums.astype(F32) * scale
    half = WEIGHT_ROWS // 2
    grad_up = jnp.concatenate([sums[C * k : C * (k + 1)] for k in range(6)], axis=1)
    grad_down = jnp.concatenate(
        [sums[half + C * k : half + C * (k + 1)].T for k in range(6)], axis=0
    )
    small = jnp.concatenate(
        [sums[WEIGHT_ROWS : WEIGHT_ROWS + 56], sums[WEIGHT_ROWS + 56 : WEIGHT_ROWS + 112, :64]],
        axis=1,
    )
    return (
        updated.reshape(fields.shape),
        grad_fields.reshape(fields.shape),
        small[:49].reshape(7, 7, C),
        small[49],
        small[50],
        grad_up,
        sums[WEIGHT_ROWS + 112 : WEIGHT_ROWS + 118].reshape(-1),
        grad_down,
    )


def solution(mesh):
    fine = Mesh(mesh.devices.reshape(4, 2, 2, 8, 2), ("y", "xl", "xh", "z", "c"))
    tiles = P(("y", "xl"), ("xh", "z", "c"), None, None, None)
    return jax.shard_map(
        on_device,
        mesh=fine,
        in_specs=(tiles, P(), P(), P(), P(), P(), P(), tiles, P(), P(), P()),
        out_specs=(tiles, tiles, P(), P(), P(), P(), P(), P()),
        check_vma=False,
    )
```

```python
import math

import jax
import jax.numpy as jnp
from jax import lax
from jax.experimental import pallas as pl
from jax.experimental.pallas import tpu as pltpu
from jax.sharding import Mesh, PartitionSpec as P

GELU_C = math.sqrt(2.0 / math.pi)
EPSILON = 1e-06
F32 = jnp.float32
BF16 = jnp.bfloat16
T = 4
S = 16
PX = S * S
C = 192
HID = 768
W = 24
DW = 32
WEIGHT_ROWS = 2 * C * HID // 128
ROWS = 2560
HALF = ROWS // 2
MIB = 1024 * 1024
VMEM_LIMIT = 60 * MIB
SLABS = 3 * T // 2
BLOCKS = 32


def gelu_pair(value):
    square = value * value
    half = 0.5 + 0.5 * jnp.tanh(value * (GELU_C + GELU_C * 0.044715 * square))
    result = value * half
    slope = half + result * (1.0 - half) * (2.0 * GELU_C + GELU_C * 6.0 * 0.044715 * square)
    return (result, slope)


def turn_of(quarter):
    on_i = jnp.where(quarter == 0, S, jnp.where(quarter == 1, -1, jnp.where(quarter == 2, -S, 1)))
    on_j = jnp.where(quarter == 0, 1, jnp.where(quarter == 1, S, jnp.where(quarter == 2, -1, -S)))
    base = jnp.where(
        quarter == 0, 0, jnp.where(quarter == 1, S - 1, jnp.where(quarter == 2, PX - 1, PX - S))
    )
    return on_i, on_j, base


SLOTS = (
    (0, S - 3, -3, 3, 19),
    (2, 0, -3, 3, 19),
    (1, 0, S - 3, 0, 3),
    (1, 0, -19, 19, 22),
    (0, S - 3, S - 3, 0, 3),
    (0, S - 3, -19, 19, 22),
    (2, 0, S - 3, 0, 3),
    (2, 0, -19, 19, 22),
)
FIRST = (0, 3, 19)
COUNT = (3, S, 3)


def slot_match(slot, quarter, transposed):
    group, row0, col0, low, high = SLOTS[slot]
    length = COUNT[group] * W
    shape = (PX, length) if transposed else (length, PX)
    along = 1 if transposed else 0
    line = (1, length) if transposed else (length, 1)
    place = lax.broadcasted_iota(jnp.int32, line, along)
    row = place // W
    col = place - row * W
    on_i, on_j, base = turn_of(quarter)
    source = on_i * (row + row0) + on_j * (col + col0) + base
    source = jnp.where((col >= low) & (col < high), source, -1)
    return (lax.broadcasted_iota(jnp.int32, shape, 1 - along) == source).astype(F32).astype(BF16)


def block_places(block):
    place = lax.broadcasted_iota(jnp.int32, (8 * S, 1), 0)
    row = place // 8
    return row, place - row * 8 + 8 * block


def matches(source):
    at = lax.broadcasted_iota(jnp.int32, (8 * S, PX), 1)
    return (at == source).astype(F32).astype(BF16)


def centre_match(block):
    row, col = block_places(block)
    return matches(jnp.where((col >= 3) & (col < S + 3), row * S + col - 3, -1))


def side_match(slot, quarter):
    _, row0, col0, low, high = SLOTS[slot]
    row, col = block_places(0 if slot == 2 else 2)
    on_i, on_j, base = turn_of(quarter)
    source = on_i * (row + row0) + on_j * (col + col0) + base
    return matches(jnp.where((col >= low) & (col < high), source, -1))


def lane_is_low():
    return lax.broadcasted_iota(jnp.int32, (1, 128), 1) < 64


def packed_slabs(x):
    first = x[:, :128]
    rest = jnp.concatenate([x[:, 128:], jnp.zeros((x.shape[0], 64), x.dtype)], axis=1)
    crossed = pltpu.roll(first, 64, 1)
    low = lane_is_low()
    return first, jnp.where(low, rest, crossed), jnp.where(low, crossed, pltpu.roll(rest, 64, 1))


def prepare_kernel(
    near_hbm,
    rot_hbm,
    owner_hbm,
    own_hbm,
    up_hbm,
    kernel_hbm,
    gain_hbm,
    bias_hbm,
    up_bias_hbm,
    where_ref,
    own_ref,
    kern,
    up_ref,
    gain_ref,
    bias_ref,
    up_bias_ref,
    near_ref,
    rot_ref,
    owner_ref,
    own_raw,
    up_raw,
    kernel_ref,
    gain_in,
    bias_in,
    up_bias_in,
    ids,
    sems,
):
    copies = [
        pltpu.make_async_copy(a, b, sems.at[k])
        for k, (a, b) in enumerate(
            (
                (near_hbm, near_ref),
                (rot_hbm, rot_ref),
                (owner_hbm, owner_ref),
                (own_hbm, own_raw),
                (up_hbm, up_raw),
                (kernel_hbm, kernel_ref),
                (gain_hbm, gain_in),
                (bias_hbm, bias_in),
                (up_bias_hbm, up_bias_in),
            )
        )
    ]
    for copy in copies:
        copy.start()
    for copy in copies:
        copy.wait()

    position = (lax.axis_index("xh") * 8 + lax.axis_index("z")) * 2 + lax.axis_index("c")
    first = position * T

    @pl.loop(0, 128, unroll=8)
    def _(q):
        at = owner_ref[q] - first

        @pl.when((at >= 0) & (at < T))
        def _():
            ids[at] = q

    for tile in range(T):
        for slot in range(8):
            row = owner_ref[near_ref[slot, ids[tile]]]
            block = lax.rem(row // T - position + 1 + BLOCKS, BLOCKS)
            where_ref[tile * 8 + slot] = block * T + lax.rem(row, T)
            where_ref[T * 8 + tile * 8 + slot] = rot_ref[slot, ids[tile]]

    own_ref[:, :, :C] = own_raw[...]
    own_ref[:, :, C:] = jnp.zeros((T, PX, 256 - C), BF16)
    for part, value in enumerate(packed_slabs(gain_in[...].reshape(1, C))):
        gain_ref[part] = value
    for part, value in enumerate(packed_slabs(bias_in[...].reshape(1, C))):
        bias_ref[part] = value
    up_bias_ref[...] = up_bias_in[...].reshape(1, HID)
    for a in range(7):
        for part, value in enumerate(packed_slabs(kernel_ref[a])):
            for b in range(7):
                tap = jnp.broadcast_to(value[b : b + 1], (8, 128))
                kern[part, 8 * (a * 7 + b) : 8 * (a * 7 + b + 1), :] = tap
    up_ref[0, :C, :] = up_raw[...]
    up_ref[0, C:, :] = jnp.zeros((64, HID), BF16)
    up_ref[1, :64, :] = jnp.zeros((64, HID), BF16)
    up_ref[1, 64:, :] = up_raw[...]


def run_prepare(*args):
    vmem = pl.BlockSpec(memory_space=pltpu.VMEM)
    smem = pl.BlockSpec(memory_space=pltpu.SMEM)
    hbm = pl.BlockSpec(memory_space=pltpu.HBM)
    return pl.pallas_call(
        prepare_kernel,
        out_shape=(
            jax.ShapeDtypeStruct((T * 16,), jnp.int32),
            jax.ShapeDtypeStruct((T, PX, 256), BF16),
            jax.ShapeDtypeStruct((3, 8 * 49, 128), F32),
            jax.ShapeDtypeStruct((2, 256, HID), BF16),
            jax.ShapeDtypeStruct((3, 1, 128), F32),
            jax.ShapeDtypeStruct((3, 1, 128), F32),
            jax.ShapeDtypeStruct((1, HID), F32),
        ),
        in_specs=[hbm] * 9,
        out_specs=(smem,) + (vmem,) * 6,
        scratch_shapes=[
            pltpu.SMEM((8, 128), jnp.int32),
            pltpu.SMEM((8, 128), jnp.int32),
            pltpu.SMEM((128,), jnp.int32),
            pltpu.VMEM((T, PX, C), BF16),
            pltpu.VMEM((C, HID), BF16),
            pltpu.VMEM((7, 7, C), F32),
            pltpu.VMEM((C,), F32),
            pltpu.VMEM((C,), F32),
            pltpu.VMEM((HID,), F32),
            pltpu.SMEM((T,), jnp.int32),
            pltpu.SemaphoreType.DMA((9,)),
        ],
        compiler_params=pltpu.CompilerParams(vmem_limit_bytes=VMEM_LIMIT),
        cost_estimate=pl.CostEstimate(flops=10**8, bytes_accessed=6 * 10**6, transcendentals=0),
    )(*args)


def forward_kernel(
    where_hbm,
    prev_hbm,
    next_hbm,
    own_hbm,
    cot_hbm,
    down_hbm,
    up_hbm,
    kern_hbm,
    gain_hbm,
    bias_hbm,
    up_bias_hbm,
    updated_hbm,
    dmix_hbm,
    send_ref,
    keep_ref,
    where_ref,
    raw,
    cot_ref,
    down_ref,
    up_ref,
    kern,
    gain_ref,
    bias_ref,
    up_bias_ref,
    out_ref,
    dmix,
    src,
    pad,
    mix,
    xhat,
    inv,
    normed,
    g_up_bias,
    g_small,
    grads_ref,
    up_ref32,
    back_ref32,
    act_ref,
    d_up_ref,
    sems,
):
    low_half = lane_is_low()
    core = lax.axis_index("c")
    copies = [
        pltpu.make_async_copy(a, b, sems.at[k])
        for k, (a, b) in enumerate(
            (
                (where_hbm, where_ref),
                (prev_hbm, raw.at[0:T]),
                (next_hbm, raw.at[T:]),
                (own_hbm, src.at[T : 2 * T]),
                (kern_hbm, kern),
                (gain_hbm, gain_ref),
                (bias_hbm, bias_ref),
                (up_hbm, up_ref),
                (down_hbm, down_ref),
                (cot_hbm, cot_ref),
                (up_bias_hbm, up_bias_ref),
            )
        )
    ]
    for copy in copies:
        copy.start()
    src[0:T, :, C:] = jnp.zeros((T, PX, 256 - C), BF16)
    src[2 * T :, :, C:] = jnp.zeros((T, PX, 256 - C), BF16)
    g_up_bias[...] = jnp.zeros_like(g_up_bias)
    g_small[...] = jnp.zeros_like(g_small)
    dmix[...] = jnp.zeros_like(dmix)
    grads_ref[...] = jnp.zeros_like(grads_ref)
    for copy in copies[:4]:
        copy.wait()
    src[0:T, :, :C] = raw[0:T]
    src[2 * T :, :, :C] = raw[T:]

    def put_rows(pair, half, start, count, value):
        rows = pl.ds(start, count)
        if half == 0:
            pad[pair * 3, rows, :] = value[:, :128]
            pad[pair * 3 + 1, rows, :] = value[:, 128:]
        else:
            pad[pair * 3 + 1, rows, :] += value[:, :128]
            pad[pair * 3 + 2, rows, :] = value[:, 128:]

    def put(pair, half, start, count, value):
        put_rows(pair, half, start, count, value if half == 0 else pltpu.roll(value, 64, 1))

    @pl.loop(0, T // 2)
    def _(pair):
        for half in range(2):
            tile = pair * 2 + half
            for group in (0, 2):
                total = None
                for slot in range(8):
                    if SLOTS[slot][0] != group:
                        continue
                    match = slot_match(slot, where_ref[T * 8 + tile * 8 + slot], False)
                    piece = jnp.dot(
                        match, src[where_ref[tile * 8 + slot]], preferred_element_type=F32
                    )
                    total = piece if total is None else total + piece
                put(pair, half, FIRST[group] * W, COUNT[group] * W, total)
            for block in range(3):
                total = jnp.dot(centre_match(block), src[T + tile], preferred_element_type=F32)
                if block != 1:
                    slot = 2 + block // 2
                    match = side_match(slot, where_ref[T * 8 + tile * 8 + slot])
                    total += jnp.dot(
                        match, src[where_ref[tile * 8 + slot]], preferred_element_type=F32
                    )
                if half == 1:
                    total = pltpu.roll(total, 64, 1)
                for i in range(S):
                    put_rows(pair, half, (i + 3) * W + 8 * block, 8, total[8 * i : 8 * i + 8])

    for copy in copies[4:7]:
        copy.wait()

    @pl.loop(0, 3 * T // 2)
    def _(slab):
        part = lax.rem(slab, 3)
        for half in range(2):
            for b in range(7):
                acc = [None] * S
                taps = [kern[part, pl.ds(8 * (a * 7 + b), 8), :] for a in range(7)]
                for m in range(S + 6):
                    x = pad[slab, pl.ds(m * W + b + 8 * half, 8), :]
                    for a in range(7):
                        i = m - a
                        if 0 <= i < S:
                            term = x * taps[a]
                            acc[i] = term if acc[i] is None else acc[i] + term
                for i in range(S):
                    rows = pl.ds(i * S + 8 * half, 8)
                    mix[slab, rows, :] = acc[i] if b == 0 else mix[slab, rows, :] + acc[i]

    def pair_means(s0, s1, s2):
        first = jnp.sum(s0 + jnp.where(low_half, s1, 0.0), axis=1, keepdims=True) * (1.0 / C)
        second = jnp.sum(s2 + jnp.where(low_half, 0.0, s1), axis=1, keepdims=True) * (1.0 / C)
        return first, jnp.where(low_half, first, second), second

    CH = 64

    @pl.loop(0, (T // 2) * (PX // CH), unroll=4)
    def _(step):
        pair = step // (PX // CH)
        rows = pl.ds(pl.multiple_of(lax.rem(step, PX // CH) * CH, CH), CH)
        slabs = [mix[pair * 3 + k, rows, :] for k in range(3)]
        means = pair_means(*slabs)
        slabs = [x - m for x, m in zip(slabs, means)]
        spreads = pair_means(*[x * x for x in slabs])
        for k in range(3):
            deviation = jnp.broadcast_to(lax.rsqrt(spreads[k] + EPSILON), (CH, 128))
            standard = slabs[k] * deviation
            inv[pair * 3 + k, rows, :] = deviation
            xhat[pair * 3 + k, rows, :] = standard
            normed[pair, rows, 128 * k : 128 * (k + 1)] = (
                standard * gain_ref[k] + bias_ref[k]
            ).astype(BF16)

    for copy in copies[7:]:
        copy.wait()

    @pl.loop(0, T // 2)
    def _(pair):
        normed_grads = []
        for half in range(2):
            tile = pair * 2 + half
            x = normed[pair, :, 128 * half : 128 * half + 256]
            x_t = jnp.transpose(x.astype(F32)).astype(BF16)
            cot = cot_ref[tile]
            cot_t = jnp.transpose(cot.astype(F32)).astype(BF16)
            branch = jnp.zeros((PX, C), F32)
            normed_grad = jnp.zeros((PX, 256), F32)
            for chunk in range(3):
                hid = slice(256 * chunk, 256 * (chunk + 1))
                up_ref32[...] = jnp.dot(x, up_ref[half, :, hid], preferred_element_type=F32)
                back_ref32[...] = jnp.dot(cot, down_ref[:, hid], preferred_element_type=F32)
                bias_sum = jnp.zeros((8, 256), F32)
                for r in range(0, PX, 16):
                    rows = slice(r, r + 16)
                    value, slope = gelu_pair(up_ref32[rows, :] + up_bias_ref[:, hid])
                    d_up = back_ref32[rows, :] * slope
                    bias_sum += d_up[:8] + d_up[8:]
                    act_ref[rows, :] = value.astype(BF16)
                    d_up_ref[rows, :] = d_up.astype(BF16)
                g_up_bias[:, hid] += bias_sum
                activation = act_ref[...]
                d_up_b = d_up_ref[...]
                branch += times_transposed(activation, down_ref[:, hid])
                down_grad = jnp.dot(cot_t, activation, preferred_element_type=F32)
                up_grad = jnp.dot(x_t, d_up_b, preferred_element_type=F32)
                for k in range(2):
                    at = C * (2 * chunk + k)
                    lanes = slice(128 * k, 128 * (k + 1))
                    grads_ref[at : at + C, :] += up_grad[64 * half : 64 * half + C, lanes]
                    at += WEIGHT_ROWS // 2
                    grads_ref[at : at + C, :] += down_grad[:, lanes]
                normed_grad += times_transposed(d_up_b, up_ref[half, :, hid])
            out_ref[tile] = (src[T + tile, :, :C].astype(F32) + branch).astype(BF16)
            normed_grads.append(normed_grad)
        mix[pair * 3] = normed_grads[0][:, :128]
        mix[pair * 3 + 1] = normed_grads[0][:, 128:] + normed_grads[1][:, :128]
        mix[pair * 3 + 2] = normed_grads[1][:, 128:]

    @pl.loop(0, (T // 2) * (PX // CH), unroll=4)
    def _(step):
        pair = step // (PX // CH)
        start = pl.multiple_of(lax.rem(step, PX // CH) * CH, CH)
        rows = pl.ds(start, CH)
        grads = [mix[pair * 3 + k, rows, :] for k in range(3)]
        standard = [xhat[pair * 3 + k, rows, :] for k in range(3)]
        for k in range(3):
            g_small[k, 8 * 49 : 8 * 50, :] += jnp.sum(
                (grads[k] * standard[k]).reshape(CH // 8, 8, 128), axis=0
            )
            g_small[k, 8 * 50 : 8 * 51, :] += jnp.sum(grads[k].reshape(CH // 8, 8, 128), axis=0)
        scaled = [grads[k] * gain_ref[k] for k in range(3)]
        means = pair_means(*scaled)
        products = pair_means(*[e * x for e, x in zip(scaled, standard)])
        for k in range(3):
            d_mixed = inv[pair * 3 + k, rows, :] * (
                scaled[k] - means[k] - standard[k] * products[k]
            )
            for r in range(CH // S):
                at = (start // S + r) * DW + 8
                dmix[pair * 3 + k, pl.ds(pl.multiple_of(at, 8), S), :] = d_mixed[r * S : (r + 1) * S]

    results = [
        pltpu.make_async_copy(out_ref, updated_hbm, sems.at[11]),
        pltpu.make_async_copy(dmix, dmix_hbm, sems.at[12]),
    ]
    for result in results:
        result.start()

    @pl.loop(0, 3 * T // 2)
    def _(slab):
        part = lax.rem(slab, 3)
        for half in range(2):
            grads = [dmix[slab, pl.ds(i * DW + 8 + 8 * half, 8), :] for i in range(S)]
            for b in range(7):
                acc = [None] * 7
                for m in range(S + 6):
                    x = pad[slab, pl.ds(m * W + b + 8 * half, 8), :]
                    for a in range(7):
                        i = m - a
                        if 0 <= i < S:
                            term = x * grads[i]
                            acc[a] = term if acc[a] is None else acc[a] + term
                for a in range(7):
                    g_small[part, 8 * (a * 7 + b) : 8 * (a * 7 + b + 1), :] += acc[a]
    sums = [jnp.sum(g_small[k].reshape(56, 8, 128), axis=1) for k in range(3)]
    crossed = pltpu.roll(jnp.where(low_half, sums[2], sums[1]), 64, 1)
    grads_ref[WEIGHT_ROWS : WEIGHT_ROWS + 56, :] = (sums[0] + crossed)
    grads_ref[WEIGHT_ROWS + 56 : WEIGHT_ROWS + 112, :] = (
        sums[1] + pltpu.roll(sums[2], 64, 1)
    )
    bias_sum = jnp.sum(g_up_bias[...], axis=0, keepdims=True)
    bias_rows = jnp.concatenate(
        [bias_sum[:, 128 * k : 128 * (k + 1)] for k in range(6)] + [jnp.zeros((10, 128), F32)],
        axis=0,
    )
    grads_ref[WEIGHT_ROWS + 112 : WEIGHT_ROWS + 128, :] = bias_rows
    send_ref[...] = grads_ref[pl.ds((1 - core) * HALF, HALF), :].astype(BF16)
    keep_ref[...] = grads_ref[pl.ds(core * HALF, HALF), :]
    for result in results:
        result.wait()


def times_transposed(x, y):
    return lax.dot_general(x, y, (((1,), (1,)), ((), ())), preferred_element_type=F32)


def run_forward(*args):
    vmem = pl.BlockSpec(memory_space=pltpu.VMEM)
    hbm = pl.BlockSpec(memory_space=pl.ANY)
    slab = pltpu.VMEM((SLABS, PX, 128), F32)
    return pl.pallas_call(
        forward_kernel,
        out_shape=(
            jax.ShapeDtypeStruct((T, PX, C), BF16),
            jax.ShapeDtypeStruct((SLABS, S * DW, 128), F32),
            jax.ShapeDtypeStruct((HALF, 128), BF16),
            jax.ShapeDtypeStruct((HALF, 128), F32),
        ),
        in_specs=[hbm] * 11,
        out_specs=(hbm, hbm, vmem, vmem),
        scratch_shapes=[
            pltpu.SMEM((T * 16,), jnp.int32),
            pltpu.VMEM((2 * T, PX, C), BF16),
            pltpu.VMEM((T, PX, C), BF16),
            pltpu.VMEM((C, HID), BF16),
            pltpu.VMEM((2, 256, HID), BF16),
            pltpu.VMEM((3, 8 * 49, 128), F32),
            pltpu.VMEM((3, 1, 128), F32),
            pltpu.VMEM((3, 1, 128), F32),
            pltpu.VMEM((1, HID), F32),
            pltpu.VMEM((T, PX, C), BF16),
            pltpu.VMEM((SLABS, S * DW, 128), F32),
            pltpu.VMEM((3 * T, PX, 256), BF16),
            pltpu.VMEM((SLABS, 22 * W, 128), F32),
            slab,
            slab,
            slab,
            pltpu.VMEM((T // 2, PX, 384), BF16),
            pltpu.VMEM((8, HID), F32),
            pltpu.VMEM((3, 8 * 56, 128), F32),
            pltpu.VMEM((ROWS, 128), F32),
            pltpu.VMEM((PX, 256), F32),
            pltpu.VMEM((PX, 256), F32),
            pltpu.VMEM((PX, 256), BF16),
            pltpu.VMEM((PX, 256), BF16),
            pltpu.SemaphoreType.DMA((13,)),
        ],
        compiler_params=pltpu.CompilerParams(vmem_limit_bytes=55 * MIB),
        cost_estimate=pl.CostEstimate(flops=4 * 10**9, bytes_accessed=8 * 10**6, transcendentals=10**6),
    )(*args)


def spread_kernel(dmix, kern, dpad):
    @pl.loop(0, SLABS)
    def _(slab):
        part = lax.rem(slab, 3)
        for third in range(3):
            for b in range(7):
                acc = [None] * (S + 6)
                taps = [kern[part, pl.ds(8 * (a * 7 + b), 8), :] for a in range(7)]
                for i in range(S):
                    x = dmix[slab, pl.ds(i * DW + 8 + 8 * third - b, 8), :]
                    for a in range(7):
                        term = x * taps[a]
                        acc[i + a] = term if acc[i + a] is None else acc[i + a] + term
                for m in range(S + 6):
                    rows = pl.ds(m * W + 8 * third, 8)
                    dpad[slab, rows, :] = acc[m] if b == 0 else dpad[slab, rows, :] + acc[m]


def run_spread(dmix, taps):
    vmem = pl.BlockSpec(memory_space=pltpu.VMEM)
    return pl.pallas_call(
        spread_kernel,
        out_shape=jax.ShapeDtypeStruct((SLABS, 22 * W, 128), F32),
        in_specs=[vmem] * 2,
        out_specs=vmem,
        compiler_params=pltpu.CompilerParams(vmem_limit_bytes=VMEM_LIMIT),
        cost_estimate=pl.CostEstimate(flops=10**9, bytes_accessed=5 * 10**6, transcendentals=0),
    )(dmix, taps)


def return_kernel(
    where_ref, dpad, cot_hbm, part_ref, to_prev_ref, to_next_ref, collected, cot_ref, sem
):
    copy = pltpu.make_async_copy(cot_hbm, cot_ref, sem)
    copy.start()
    collected[...] = jnp.zeros_like(collected)

    @pl.loop(0, T // 2)
    def _(pair):
        for half in range(2):
            tile = pair * 2 + half
            for slot in range(8):
                group = SLOTS[slot][0]
                rows = pl.ds(FIRST[group] * W, COUNT[group] * W)
                border = jnp.concatenate(
                    [dpad[pair * 3 + half + k, rows, :] for k in range(2)], axis=1
                ).astype(BF16)
                match = slot_match(slot, where_ref[T * 8 + tile * 8 + slot], True)
                piece = jnp.dot(match, border, preferred_element_type=F32)
                if half == 1:
                    piece = pltpu.roll(piece, 192, 1)
                collected[where_ref[tile * 8 + slot]] += piece

    to_prev_ref[...] = collected[0:T, :, :C].astype(BF16)
    to_next_ref[...] = collected[2 * T :, :, :C].astype(BF16)
    copy.wait()

    @pl.loop(0, T // 2)
    def _(pair):
        for half in range(2):
            tile = pair * 2 + half
            for i in range(S):
                rows = slice(i * S, (i + 1) * S)
                centre = jnp.concatenate(
                    [dpad[pair * 3 + half + k, pl.ds((i + 3) * W + 3, S), :] for k in range(2)],
                    axis=1,
                )
                if half == 1:
                    centre = pltpu.roll(centre, 192, 1)
                part_ref[tile, rows, :] = (
                    cot_ref[tile, rows, :].astype(F32)
                    + centre[:, :C]
                    + collected[T + tile, rows, :C]
                )


def run_return(where, dpad, cot):
    vmem = pl.BlockSpec(memory_space=pltpu.VMEM)
    smem = pl.BlockSpec(memory_space=pltpu.SMEM)
    tile = (T, PX, C)
    return pl.pallas_call(
        return_kernel,
        out_shape=(
            jax.ShapeDtypeStruct(tile, F32),
            jax.ShapeDtypeStruct(tile, BF16),
            jax.ShapeDtypeStruct(tile, BF16),
        ),
        in_specs=[smem, vmem, pl.BlockSpec(memory_space=pltpu.HBM)],
        out_specs=(vmem,) * 3,
        scratch_shapes=[
            pltpu.VMEM((3 * T, PX, 256), F32),
            pltpu.VMEM((T, PX, C), BF16),
            pltpu.SemaphoreType.DMA,
        ],
        compiler_params=pltpu.CompilerParams(vmem_limit_bytes=VMEM_LIMIT),
        cost_estimate=pl.CostEstimate(flops=10**9, bytes_accessed=5 * 10**6, transcendentals=0),
    )(where, dpad, cot)


def finish_kernel(
    core_ref, mine_ref, other_ref, up_out, down_out, kernel_out, gain_out, bias_out, up_bias_out, halves
):
    scale = 1.0 / math.sqrt(8 * BLOCKS * T * PX)
    core = core_ref[0]
    halves[core] = mine_ref[...]
    halves[1 - core] = other_ref[...]

    def rows(start, count):
        side, at = divmod(start, HALF)
        if at + count <= HALF:
            return halves[side, at : at + count, :].astype(F32) * scale
        split = HALF - at
        return jnp.concatenate([rows(start, split), rows(start + split, count - split)], axis=0)

    for k in range(HID // 128):
        up_out[:, 128 * k : 128 * (k + 1)] = rows(C * k, C)
        down_out[:, 128 * k : 128 * (k + 1)] = rows(WEIGHT_ROWS // 2 + C * k, C)
    small = jnp.concatenate(
        [rows(WEIGHT_ROWS, 56), rows(WEIGHT_ROWS + 56, 56)[:, :64]], axis=1
    )
    for a in range(7):
        kernel_out[a] = small[7 * a : 7 * (a + 1)]
    gain_out[...] = small[49:50].reshape(C)
    bias_out[...] = small[50:51].reshape(C)
    bias = rows(WEIGHT_ROWS + 112, 16)
    for k in range(HID // 128):
        up_bias_out[128 * k : 128 * (k + 1)] = bias[k : k + 1].reshape(128)


def run_finish(core, mine, other):
    vmem = pl.BlockSpec(memory_space=pltpu.VMEM)
    smem = pl.BlockSpec(memory_space=pltpu.SMEM)
    return pl.pallas_call(
        finish_kernel,
        out_shape=(
            jax.ShapeDtypeStruct((C, HID), F32),
            jax.ShapeDtypeStruct((C, HID), F32),
            jax.ShapeDtypeStruct((7, 7, C), F32),
            jax.ShapeDtypeStruct((C,), F32),
            jax.ShapeDtypeStruct((C,), F32),
            jax.ShapeDtypeStruct((HID,), F32),
        ),
        in_specs=[smem, vmem, vmem],
        out_specs=(vmem,) * 6,
        scratch_shapes=[pltpu.VMEM((2, HALF, 128), BF16)],
        compiler_params=pltpu.CompilerParams(vmem_limit_bytes=8 * MIB),
        cost_estimate=pl.CostEstimate(flops=10**6, bytes_accessed=2 * 10**6, transcendentals=0),
    )(core, mine, other)


def shared_with(x, axes, count):
    return lax.all_to_all(jnp.broadcast_to(x[None], (count,) + x.shape), axes, 0, 0)


def total_of(x):
    return jnp.sum(x.astype(F32), axis=0)


def on_device(
    fields,
    depth_kernel,
    layer_norm_gain,
    layer_norm_bias,
    up_weight,
    up_bias,
    down_weight,
    cotangent,
    neighbours,
    rotation,
    tile_owner,
):
    around = ("xh", "z", "c")
    plane = ("y", "xl", "xh")
    swap = [(0, 1), (1, 0)]
    to_right = [(i, (i + 1) % BLOCKS) for i in range(BLOCKS)]
    to_left = [((i + 1) % BLOCKS, i) for i in range(BLOCKS)]
    own = fields.reshape(T, PX, C)
    cot = cotangent.reshape(T, PX, C)
    prev = lax.ppermute(own, around, to_right)
    nxt = lax.ppermute(own, around, to_left)
    where, wide, taps, up, gain, bias, up_bias = run_prepare(
        neighbours.T,
        rotation.T,
        tile_owner,
        own,
        up_weight,
        depth_kernel,
        layer_norm_gain,
        layer_norm_bias,
        up_bias,
    )
    updated, dmix, send, keep = run_forward(
        where, prev, nxt, wide, cot, down_weight.T, up, taps, gain, bias, up_bias
    )
    mine = (keep + lax.ppermute(send, "c", swap).astype(F32)).astype(BF16)
    dmix, mine = lax.optimization_barrier((dmix, mine))
    mine = lax.all_to_all(mine.reshape(16, HALF // 16, 128), plane, 0, 0)
    dpad = run_spread(dmix, taps)
    dpad, mine = lax.optimization_barrier((dpad, mine))
    mine = total_of(mine).astype(BF16)
    dpad, mine = lax.optimization_barrier((dpad, mine))
    mine = shared_with(mine, "z", 8)
    part, to_prev, to_next = run_return(where, dpad, cot)
    mine, to_prev, to_next = lax.optimization_barrier((mine, to_prev, to_next))
    from_right = lax.ppermute(to_prev, around, to_left)
    from_left = lax.ppermute(to_next, around, to_right)
    mine = total_of(mine).astype(BF16)
    mine = shared_with(mine, plane, 16)
    grad_fields = (part + from_right.astype(F32) + from_left.astype(F32)).astype(BF16)
    mine, grad_fields = lax.optimization_barrier((mine, grad_fields))
    mine = mine.reshape(HALF, 128)
    other = lax.ppermute(mine, "c", swap)
    core = lax.axis_index("c").astype(jnp.int32).reshape(1)
    grad_up, grad_down_t, grad_kernel, grad_gain, grad_bias, grad_up_bias = run_finish(
        core, mine, other
    )
    return (
        updated.reshape(fields.shape),
        grad_fields.reshape(fields.shape),
        grad_kernel,
        grad_gain,
        grad_bias,
        grad_up,
        grad_up_bias,
        grad_down_t.T,
    )


def solution(mesh):
    fine = Mesh(mesh.devices.reshape(4, 2, 2, 8, 2), ("y", "xl", "xh", "z", "c"))
    tiles = P(("y", "xl"), ("xh", "z", "c"), None, None, None)
    return jax.shard_map(
        on_device,
        mesh=fine,
        in_specs=(tiles, P(), P(), P(), P(), P(), P(), tiles, P(), P(), P()),
        out_specs=(tiles, tiles, P(), P(), P(), P(), P(), P()),
        check_vma=False,
    )
```

```python
import math

import jax
import jax.numpy as jnp
from jax import lax
from jax.experimental import pallas as pl
from jax.experimental.pallas import tpu as pltpu
from jax.sharding import Mesh, PartitionSpec as P

GELU_C = math.sqrt(2.0 / math.pi)
EPSILON = 1e-06
F32 = jnp.float32
BF16 = jnp.bfloat16
T = 4
S = 16
PX = S * S
C = 192
HID = 768
W = 24
DW = 32
WEIGHT_ROWS = 2 * C * HID // 128
ROWS = 2560
HALF = ROWS // 2
MIB = 1024 * 1024
SLABS = 3 * T // 2
BLOCKS = 32


def gelu_pair(value):
    square = value * value
    half = 0.5 + 0.5 * jnp.tanh(value * (GELU_C + GELU_C * 0.044715 * square))
    result = value * half
    slope = half + result * (1.0 - half) * (2.0 * GELU_C + GELU_C * 6.0 * 0.044715 * square)
    return (result, slope)


def turn_of(quarter):
    on_i = jnp.where(quarter == 0, S, jnp.where(quarter == 1, -1, jnp.where(quarter == 2, -S, 1)))
    on_j = jnp.where(quarter == 0, 1, jnp.where(quarter == 1, S, jnp.where(quarter == 2, -1, -S)))
    base = jnp.where(
        quarter == 0, 0, jnp.where(quarter == 1, S - 1, jnp.where(quarter == 2, PX - 1, PX - S))
    )
    return on_i, on_j, base


SLOTS = (
    (0, S - 3, -3, 3, 19),
    (2, 0, -3, 3, 19),
    (1, 0, S - 3, 0, 3),
    (1, 0, -19, 19, 22),
    (0, S - 3, S - 3, 0, 3),
    (0, S - 3, -19, 19, 22),
    (2, 0, S - 3, 0, 3),
    (2, 0, -19, 19, 22),
)
FIRST = (0, 3, 19)
COUNT = (3, S, 3)


def slot_match(slot, quarter, transposed):
    group, row0, col0, low, high = SLOTS[slot]
    length = COUNT[group] * W
    shape = (PX, length) if transposed else (length, PX)
    along = 1 if transposed else 0
    line = (1, length) if transposed else (length, 1)
    place = lax.broadcasted_iota(jnp.int32, line, along)
    row = place // W
    col = place - row * W
    on_i, on_j, base = turn_of(quarter)
    source = on_i * (row + row0) + on_j * (col + col0) + base
    source = jnp.where((col >= low) & (col < high), source, -1)
    return (lax.broadcasted_iota(jnp.int32, shape, 1 - along) == source).astype(F32).astype(BF16)


def block_places(block):
    place = lax.broadcasted_iota(jnp.int32, (8 * S, 1), 0)
    row = place // 8
    return row, place - row * 8 + 8 * block


def matches(source):
    at = lax.broadcasted_iota(jnp.int32, (8 * S, PX), 1)
    return (at == source).astype(F32).astype(BF16)


def centre_match(block):
    row, col = block_places(block)
    return matches(jnp.where((col >= 3) & (col < S + 3), row * S + col - 3, -1))


def side_match(slot, quarter):
    _, row0, col0, low, high = SLOTS[slot]
    row, col = block_places(0 if slot == 2 else 2)
    on_i, on_j, base = turn_of(quarter)
    source = on_i * (row + row0) + on_j * (col + col0) + base
    return matches(jnp.where((col >= low) & (col < high), source, -1))


def lane_is_low():
    return lax.broadcasted_iota(jnp.int32, (1, 128), 1) < 64


def packed_slabs(x):
    first = x[:, :128]
    rest = jnp.concatenate([x[:, 128:], jnp.zeros((x.shape[0], 64), x.dtype)], axis=1)
    crossed = pltpu.roll(first, 64, 1)
    low = lane_is_low()
    return first, jnp.where(low, rest, crossed), jnp.where(low, crossed, pltpu.roll(rest, 64, 1))


def prepare_kernel(
    table_ref,
    vector_ref,
    own_hbm,
    cot_hbm,
    up_hbm,
    down_hbm,
    kernel_hbm,
    where_ref,
    own_ref,
    cot_ref,
    up_ref,
    down_ref,
    kern,
    gain_ref,
    bias_ref,
    up_bias_ref,
    ids,
    own_raw,
    kernel_ref,
    sems,
):
    copies = [
        pltpu.make_async_copy(a, b, sems.at[k])
        for k, (a, b) in enumerate(
            (
                (kernel_hbm, kernel_ref),
                (own_hbm, own_raw),
                (up_hbm, up_ref),
                (cot_hbm, cot_ref),
                (down_hbm, down_ref),
            )
        )
    ]
    for copy in copies:
        copy.start()

    position = (lax.axis_index("xh") * 8 + lax.axis_index("z")) * 2 + lax.axis_index("c")
    first = position * T

    @pl.loop(0, 128, unroll=8)
    def _(q):
        at = table_ref[16, q] - first

        @pl.when((at >= 0) & (at < T))
        def _():
            ids[at] = q

    for tile in range(T):
        for slot in range(8):
            row = table_ref[16, table_ref[slot, ids[tile]]]
            block = lax.rem(row // T - position + 1 + BLOCKS, BLOCKS)
            where_ref[tile * 8 + slot] = block * T + lax.rem(row, T)
            where_ref[T * 8 + tile * 8 + slot] = table_ref[8 + slot, ids[tile]]

    own_ref[:, :, C:] = jnp.zeros((T, PX, 256 - C), BF16)
    for part, value in enumerate(packed_slabs(vector_ref[:, :C])):
        gain_ref[part] = value
    for part, value in enumerate(packed_slabs(vector_ref[:, 256 : 256 + C])):
        bias_ref[part] = value
    up_bias_ref[...] = vector_ref[:, 512:]
    copies[0].wait()
    for a in range(7):
        for part, value in enumerate(packed_slabs(kernel_ref[a])):
            kern[part, 8 * a : 8 * a + 7, :] = value
    copies[1].wait()
    own_ref[:, :, :C] = own_raw[...]
    for copy in copies[2:]:
        copy.wait()


def run_prepare(*args):
    vmem = pl.BlockSpec(memory_space=pltpu.VMEM)
    smem = pl.BlockSpec(memory_space=pltpu.SMEM)
    return pl.pallas_call(
        prepare_kernel,
        out_shape=(
            jax.ShapeDtypeStruct((T * 16,), jnp.int32),
            jax.ShapeDtypeStruct((T, PX, 256), BF16),
            jax.ShapeDtypeStruct((T, PX, C), BF16),
            jax.ShapeDtypeStruct((C, HID), BF16),
            jax.ShapeDtypeStruct((C, HID), BF16),
            jax.ShapeDtypeStruct((3, 56, 128), F32),
            jax.ShapeDtypeStruct((3, 1, 128), F32),
            jax.ShapeDtypeStruct((3, 1, 128), F32),
            jax.ShapeDtypeStruct((1, HID), F32),
        ),
        in_specs=[smem, vmem] + [pl.BlockSpec(memory_space=pl.ANY)] * 5,
        out_specs=(smem,) + (vmem,) * 8,
        scratch_shapes=[
            pltpu.SMEM((T,), jnp.int32),
            pltpu.VMEM((T, PX, C), BF16),
            pltpu.VMEM((7, 7, C), F32),
            pltpu.SemaphoreType.DMA((5,)),
        ],
        compiler_params=pltpu.CompilerParams(vmem_limit_bytes=52736 * 1024),
        cost_estimate=pl.CostEstimate(flops=10**8, bytes_accessed=6 * 10**6, transcendentals=0),
    )(*args)


def repeat_taps(taps_ref, kern):
    for part in range(3):
        for a in range(7):
            for b in range(7):
                at = 8 * (a * 7 + b)
                tap = taps_ref[part, 8 * a + b : 8 * a + b + 1, :]
                kern[part, at : at + 8, :] = jnp.broadcast_to(tap, (8, 128))


def forward_kernel(
    where_ref,
    prev_ref,
    next_ref,
    own_ref,
    cot_ref,
    up_raw,
    down_ref,
    taps_ref,
    gain_ref,
    bias_ref,
    up_bias_ref,
    updated_hbm,
    dmix,
    send_ref,
    keep_ref,
    out_ref,
    src,
    pad,
    mix,
    xhat,
    inv,
    normed,
    g_up_bias,
    g_small,
    grads_ref,
    up_ref32,
    back_ref32,
    act_ref,
    d_up_ref,
    up_ref,
    kern,
    sem,
):
    low_half = lane_is_low()
    core = lax.axis_index("c")
    src[0:T, :, C:] = jnp.zeros((T, PX, 256 - C), BF16)
    src[2 * T :, :, C:] = jnp.zeros((T, PX, 256 - C), BF16)
    src[0:T, :, :C] = prev_ref[...]
    src[T : 2 * T] = own_ref[...]
    up_ref[0, :C, :] = up_raw[...]
    up_ref[0, C:, :] = jnp.zeros((64, HID), BF16)
    up_ref[1, :64, :] = jnp.zeros((64, HID), BF16)
    up_ref[1, 64:, :] = up_raw[...]
    repeat_taps(taps_ref, kern)
    src[2 * T :, :, :C] = next_ref[...]
    g_up_bias[...] = jnp.zeros_like(g_up_bias)
    g_small[...] = jnp.zeros_like(g_small)
    dmix[...] = jnp.zeros_like(dmix)
    grads_ref[...] = jnp.zeros_like(grads_ref)
    def put_rows(pair, half, start, count, value):
        rows = pl.ds(start, count)
        if half == 0:
            pad[pair * 3, rows, :] = value[:, :128]
            pad[pair * 3 + 1, rows, :] = value[:, 128:]
        else:
            pad[pair * 3 + 1, rows, :] += value[:, :128]
            pad[pair * 3 + 2, rows, :] = value[:, 128:]

    def put(pair, half, start, count, value):
        put_rows(pair, half, start, count, value if half == 0 else pltpu.roll(value, 64, 1))

    @pl.loop(0, T // 2)
    def _(pair):
        for half in range(2):
            tile = pair * 2 + half
            for group in (0, 2):
                total = None
                for slot in range(8):
                    if SLOTS[slot][0] != group:
                        continue
                    match = slot_match(slot, where_ref[T * 8 + tile * 8 + slot], False)
                    piece = jnp.dot(
                        match, src[where_ref[tile * 8 + slot]], preferred_element_type=F32
                    )
                    total = piece if total is None else total + piece
                put(pair, half, FIRST[group] * W, COUNT[group] * W, total)
            for block in range(3):
                total = jnp.dot(centre_match(block), src[T + tile], preferred_element_type=F32)
                if block != 1:
                    slot = 2 + block // 2
                    match = side_match(slot, where_ref[T * 8 + tile * 8 + slot])
                    total += jnp.dot(
                        match, src[where_ref[tile * 8 + slot]], preferred_element_type=F32
                    )
                if half == 1:
                    total = pltpu.roll(total, 64, 1)
                for i in range(S):
                    put_rows(pair, half, (i + 3) * W + 8 * block, 8, total[8 * i : 8 * i + 8])

    @pl.loop(0, 3 * T // 2)
    def _(slab):
        part = lax.rem(slab, 3)
        for half in range(2):
            for b in range(7):
                acc = [None] * S
                taps = [kern[part, pl.ds(8 * (a * 7 + b), 8), :] for a in range(7)]
                for m in range(S + 6):
                    x = pad[slab, pl.ds(m * W + b + 8 * half, 8), :]
                    for a in range(7):
                        i = m - a
                        if 0 <= i < S:
                            term = x * taps[a]
                            acc[i] = term if acc[i] is None else acc[i] + term
                for i in range(S):
                    rows = pl.ds(i * S + 8 * half, 8)
                    mix[slab, rows, :] = acc[i] if b == 0 else mix[slab, rows, :] + acc[i]

    def pair_means(s0, s1, s2):
        first = jnp.sum(s0 + jnp.where(low_half, s1, 0.0), axis=1, keepdims=True) * (1.0 / C)
        second = jnp.sum(s2 + jnp.where(low_half, 0.0, s1), axis=1, keepdims=True) * (1.0 / C)
        return first, jnp.where(low_half, first, second), second

    CH = 64

    @pl.loop(0, (T // 2) * (PX // CH), unroll=4)
    def _(step):
        pair = step // (PX // CH)
        rows = pl.ds(pl.multiple_of(lax.rem(step, PX // CH) * CH, CH), CH)
        slabs = [mix[pair * 3 + k, rows, :] for k in range(3)]
        means = pair_means(*slabs)
        slabs = [x - m for x, m in zip(slabs, means)]
        spreads = pair_means(*[x * x for x in slabs])
        for k in range(3):
            deviation = jnp.broadcast_to(lax.rsqrt(spreads[k] + EPSILON), (CH, 128))
            standard = slabs[k] * deviation
            inv[pair * 3 + k, rows, :] = deviation
            xhat[pair * 3 + k, rows, :] = standard
            normed[pair, rows, 128 * k : 128 * (k + 1)] = (
                standard * gain_ref[k] + bias_ref[k]
            ).astype(BF16)

    def enter(step, half, chunk, x, cot):
        hid = slice(256 * chunk, 256 * (chunk + 1))
        up_ref32[step % 3] = jnp.dot(x, up_ref[half, :, hid], preferred_element_type=F32)
        back_ref32[step % 3] = jnp.dot(cot, down_ref[:, hid], preferred_element_type=F32)

    @pl.loop(0, T // 2, unroll=2)
    def _(pair):
        xs = [normed[pair, :, 128 * half : 128 * half + 256] for half in range(2)]
        cots = [cot_ref[pair * 2 + half] for half in range(2)]
        steps = [(half, chunk) for half in range(2) for chunk in range(3)]
        enter(0, 0, 0, xs[0], cots[0])
        for step, (half, chunk) in enumerate(steps):
            if step + 1 < len(steps):
                after = steps[step + 1]
                enter(step + 1, *after, xs[after[0]], cots[after[0]])
            hid = slice(256 * chunk, 256 * (chunk + 1))
            if chunk == 0:
                x_t = jnp.transpose(xs[half].astype(F32)).astype(BF16)
                cot_t = jnp.transpose(cots[half].astype(F32)).astype(BF16)
                branch = jnp.zeros((PX, C), F32)
                normed_grad = jnp.zeros((PX, 256), F32)
            slot = step % 3
            bias_sum = jnp.zeros((8, 256), F32)
            for r in range(0, PX, 16):
                rows = slice(r, r + 16)
                value, slope = gelu_pair(up_ref32[slot, rows, :] + up_bias_ref[:, hid])
                d_up = back_ref32[slot, rows, :] * slope
                bias_sum += d_up[:8] + d_up[8:]
                act_ref[slot, rows, :] = value.astype(BF16)
                d_up_ref[slot, rows, :] = d_up.astype(BF16)
            g_up_bias[:, hid] += bias_sum
            activation = act_ref[slot]
            d_up_b = d_up_ref[slot]
            branch += times_transposed(activation, down_ref[:, hid])
            down_grad = jnp.dot(cot_t, activation, preferred_element_type=F32)
            up_grad = jnp.dot(x_t, d_up_b, preferred_element_type=F32)
            for k in range(2):
                at = C * (2 * chunk + k)
                lanes = slice(128 * k, 128 * (k + 1))
                grads_ref[at : at + C, :] += up_grad[64 * half : 64 * half + C, lanes]
                at += WEIGHT_ROWS // 2
                grads_ref[at : at + C, :] += down_grad[:, lanes]
            normed_grad += times_transposed(d_up_b, up_ref[half, :, hid])
            if chunk == 2:
                tile = pair * 2 + half
                own = src[T + tile, :, :C].astype(F32)
                out_ref[tile] = (own + branch).astype(BF16)
                if half == 0:
                    mix[pair * 3] = normed_grad[:, :128]
                    mix[pair * 3 + 1] = normed_grad[:, 128:]
                else:
                    mix[pair * 3 + 1] += normed_grad[:, :128]
                    mix[pair * 3 + 2] = normed_grad[:, 128:]

    @pl.loop(0, (T // 2) * (PX // CH), unroll=4)
    def _(step):
        pair = step // (PX // CH)
        start = pl.multiple_of(lax.rem(step, PX // CH) * CH, CH)
        rows = pl.ds(start, CH)
        grads = [mix[pair * 3 + k, rows, :] for k in range(3)]
        standard = [xhat[pair * 3 + k, rows, :] for k in range(3)]
        for k in range(3):
            g_small[k, 8 * 49 : 8 * 50, :] += jnp.sum(
                (grads[k] * standard[k]).reshape(CH // 8, 8, 128), axis=0
            )
            g_small[k, 8 * 50 : 8 * 51, :] += jnp.sum(grads[k].reshape(CH // 8, 8, 128), axis=0)
        scaled = [grads[k] * gain_ref[k] for k in range(3)]
        means = pair_means(*scaled)
        products = pair_means(*[e * x for e, x in zip(scaled, standard)])
        for k in range(3):
            d_mixed = inv[pair * 3 + k, rows, :] * (
                scaled[k] - means[k] - standard[k] * products[k]
            )
            for r in range(CH // S):
                at = (start // S + r) * DW + 8
                dmix[pair * 3 + k, pl.ds(pl.multiple_of(at, 8), S), :] = d_mixed[r * S : (r + 1) * S]

    result = pltpu.make_async_copy(out_ref, updated_hbm, sem)
    result.start()

    @pl.loop(0, 3 * T // 2)
    def _(slab):
        part = lax.rem(slab, 3)
        for half in range(2):
            grads = [dmix[slab, pl.ds(i * DW + 8 + 8 * half, 8), :] for i in range(S)]
            for b in range(7):
                acc = [None] * 7
                for m in range(S + 6):
                    x = pad[slab, pl.ds(m * W + b + 8 * half, 8), :]
                    for a in range(7):
                        i = m - a
                        if 0 <= i < S:
                            term = x * grads[i]
                            acc[a] = term if acc[a] is None else acc[a] + term
                for a in range(7):
                    g_small[part, 8 * (a * 7 + b) : 8 * (a * 7 + b + 1), :] += acc[a]
    sums = [jnp.sum(g_small[k].reshape(56, 8, 128), axis=1) for k in range(3)]
    crossed = pltpu.roll(jnp.where(low_half, sums[2], sums[1]), 64, 1)
    grads_ref[WEIGHT_ROWS : WEIGHT_ROWS + 56, :] = (sums[0] + crossed)
    grads_ref[WEIGHT_ROWS + 56 : WEIGHT_ROWS + 112, :] = (
        sums[1] + pltpu.roll(sums[2], 64, 1)
    )
    bias_sum = jnp.sum(g_up_bias[...], axis=0, keepdims=True)
    bias_rows = jnp.concatenate(
        [bias_sum[:, 128 * k : 128 * (k + 1)] for k in range(6)] + [jnp.zeros((10, 128), F32)],
        axis=0,
    )
    grads_ref[WEIGHT_ROWS + 112 : WEIGHT_ROWS + 128, :] = bias_rows
    send_ref[...] = grads_ref[pl.ds((1 - core) * HALF, HALF), :].astype(BF16)
    keep_ref[...] = grads_ref[pl.ds(core * HALF, HALF), :]
    result.wait()


def times_transposed(x, y):
    return lax.dot_general(x, y, (((1,), (1,)), ((), ())), preferred_element_type=F32)


def run_forward(*args):
    vmem = pl.BlockSpec(memory_space=pltpu.VMEM)
    smem = pl.BlockSpec(memory_space=pltpu.SMEM)
    slab = pltpu.VMEM((SLABS, PX, 128), F32)
    return pl.pallas_call(
        forward_kernel,
        out_shape=(
            jax.ShapeDtypeStruct((T, PX, C), BF16),
            jax.ShapeDtypeStruct((SLABS, S * DW, 128), F32),
            jax.ShapeDtypeStruct((HALF, 128), BF16),
            jax.ShapeDtypeStruct((HALF, 128), F32),
        ),
        in_specs=[smem] + [vmem] * 10,
        out_specs=(pl.BlockSpec(memory_space=pl.ANY), vmem, vmem, vmem),
        scratch_shapes=[
            pltpu.VMEM((T, PX, C), BF16),
            pltpu.VMEM((3 * T, PX, 256), BF16),
            pltpu.VMEM((SLABS, 22 * W, 128), F32),
            slab,
            slab,
            slab,
            pltpu.VMEM((T // 2, PX, 384), BF16),
            pltpu.VMEM((8, HID), F32),
            pltpu.VMEM((3, 8 * 56, 128), F32),
            pltpu.VMEM((ROWS, 128), F32),
            pltpu.VMEM((3, PX, 256), F32),
            pltpu.VMEM((3, PX, 256), F32),
            pltpu.VMEM((3, PX, 256), BF16),
            pltpu.VMEM((3, PX, 256), BF16),
            pltpu.VMEM((2, 256, HID), BF16),
            pltpu.VMEM((3, 8 * 49, 128), F32),
            pltpu.SemaphoreType.DMA,
        ],
        compiler_params=pltpu.CompilerParams(vmem_limit_bytes=24 * MIB),
        cost_estimate=pl.CostEstimate(flops=4 * 10**9, bytes_accessed=8 * 10**6, transcendentals=10**6),
    )(*args)


def spread_kernel(dmix, taps_ref, dpad, kern):
    repeat_taps(taps_ref, kern)

    @pl.loop(0, SLABS)
    def _(slab):
        part = lax.rem(slab, 3)
        for third in range(3):
            for b in range(7):
                acc = [None] * (S + 6)
                taps = [kern[part, pl.ds(8 * (a * 7 + b), 8), :] for a in range(7)]
                for i in range(S):
                    x = dmix[slab, pl.ds(i * DW + 8 + 8 * third - b, 8), :]
                    for a in range(7):
                        term = x * taps[a]
                        acc[i + a] = term if acc[i + a] is None else acc[i + a] + term
                for m in range(S + 6):
                    rows = pl.ds(m * W + 8 * third, 8)
                    dpad[slab, rows, :] = acc[m] if b == 0 else dpad[slab, rows, :] + acc[m]


def run_spread(dmix, taps):
    vmem = pl.BlockSpec(memory_space=pltpu.VMEM)
    return pl.pallas_call(
        spread_kernel,
        out_shape=jax.ShapeDtypeStruct((SLABS, 22 * W, 128), F32),
        in_specs=[vmem] * 2,
        out_specs=vmem,
        scratch_shapes=[pltpu.VMEM((3, 8 * 49, 128), F32)],
        compiler_params=pltpu.CompilerParams(vmem_limit_bytes=12 * MIB),
        cost_estimate=pl.CostEstimate(flops=10**9, bytes_accessed=5 * 10**6, transcendentals=0),
    )(dmix, taps)


def return_kernel(where_ref, dpad, cot_ref, part_ref, to_prev_ref, to_next_ref, collected):
    collected[...] = jnp.zeros_like(collected)

    @pl.loop(0, T // 2)
    def _(pair):
        for half in range(2):
            tile = pair * 2 + half
            for slot in range(8):
                group = SLOTS[slot][0]
                rows = pl.ds(FIRST[group] * W, COUNT[group] * W)
                border = jnp.concatenate(
                    [dpad[pair * 3 + half + k, rows, :] for k in range(2)], axis=1
                ).astype(BF16)
                match = slot_match(slot, where_ref[T * 8 + tile * 8 + slot], True)
                piece = jnp.dot(match, border, preferred_element_type=F32)
                if half == 1:
                    piece = pltpu.roll(piece, 192, 1)
                collected[where_ref[tile * 8 + slot]] += piece

    to_prev_ref[...] = collected[0:T, :, :C].astype(BF16)
    to_next_ref[...] = collected[2 * T :, :, :C].astype(BF16)

    @pl.loop(0, T // 2)
    def _(pair):
        for half in range(2):
            tile = pair * 2 + half
            for i in range(S):
                rows = slice(i * S, (i + 1) * S)
                centre = jnp.concatenate(
                    [dpad[pair * 3 + half + k, pl.ds((i + 3) * W + 3, S), :] for k in range(2)],
                    axis=1,
                )
                if half == 1:
                    centre = pltpu.roll(centre, 192, 1)
                part_ref[tile, rows, :] = (
                    cot_ref[tile, rows, :].astype(F32)
                    + centre[:, :C]
                    + collected[T + tile, rows, :C]
                )


def run_return(where, dpad, cot):
    vmem = pl.BlockSpec(memory_space=pltpu.VMEM)
    smem = pl.BlockSpec(memory_space=pltpu.SMEM)
    tile = (T, PX, C)
    return pl.pallas_call(
        return_kernel,
        out_shape=(
            jax.ShapeDtypeStruct(tile, F32),
            jax.ShapeDtypeStruct(tile, BF16),
            jax.ShapeDtypeStruct(tile, BF16),
        ),
        in_specs=[smem, vmem, vmem],
        out_specs=(vmem,) * 3,
        scratch_shapes=[pltpu.VMEM((3 * T, PX, 256), F32)],
        compiler_params=pltpu.CompilerParams(vmem_limit_bytes=16 * MIB),
        cost_estimate=pl.CostEstimate(flops=10**9, bytes_accessed=5 * 10**6, transcendentals=0),
    )(where, dpad, cot)


def finish_kernel(
    core_ref, mine_ref, other_ref, up_out, down_out, kernel_out, gain_out, bias_out, up_bias_out, halves
):
    scale = 1.0 / math.sqrt(8 * BLOCKS * T * PX)
    core = core_ref[0]
    halves[core] = mine_ref[...]
    halves[1 - core] = other_ref[...]

    def rows(start, count):
        side, at = divmod(start, HALF)
        if at + count <= HALF:
            return halves[side, at : at + count, :].astype(F32) * scale
        split = HALF - at
        return jnp.concatenate([rows(start, split), rows(start + split, count - split)], axis=0)

    for k in range(HID // 128):
        up_out[:, 128 * k : 128 * (k + 1)] = rows(C * k, C)
        down_out[:, 128 * k : 128 * (k + 1)] = rows(WEIGHT_ROWS // 2 + C * k, C)
    small = jnp.concatenate(
        [rows(WEIGHT_ROWS, 56), rows(WEIGHT_ROWS + 56, 56)[:, :64]], axis=1
    )
    for a in range(7):
        kernel_out[a] = small[7 * a : 7 * (a + 1)]
    gain_out[...] = small[49:50].reshape(C)
    bias_out[...] = small[50:51].reshape(C)
    bias = rows(WEIGHT_ROWS + 112, 16)
    for k in range(HID // 128):
        up_bias_out[128 * k : 128 * (k + 1)] = bias[k : k + 1].reshape(128)


def run_finish(core, mine, other):
    vmem = pl.BlockSpec(memory_space=pltpu.VMEM)
    smem = pl.BlockSpec(memory_space=pltpu.SMEM)
    return pl.pallas_call(
        finish_kernel,
        out_shape=(
            jax.ShapeDtypeStruct((C, HID), F32),
            jax.ShapeDtypeStruct((C, HID), F32),
            jax.ShapeDtypeStruct((7, 7, C), F32),
            jax.ShapeDtypeStruct((C,), F32),
            jax.ShapeDtypeStruct((C,), F32),
            jax.ShapeDtypeStruct((HID,), F32),
        ),
        in_specs=[smem, vmem, vmem],
        out_specs=(vmem,) * 6,
        scratch_shapes=[pltpu.VMEM((2, HALF, 128), BF16)],
        compiler_params=pltpu.CompilerParams(vmem_limit_bytes=8 * MIB),
        cost_estimate=pl.CostEstimate(flops=10**6, bytes_accessed=2 * 10**6, transcendentals=0),
    )(core, mine, other)


def shared_with(x, axes, count):
    return lax.all_to_all(jnp.broadcast_to(x[None], (count,) + x.shape), axes, 0, 0)


def total_of(x):
    return jnp.sum(x.astype(F32), axis=0)


def on_device(
    fields,
    depth_kernel,
    layer_norm_gain,
    layer_norm_bias,
    up_weight,
    up_bias,
    down_weight,
    cotangent,
    neighbours,
    rotation,
    tile_owner,
):
    around = ("xh", "z", "c")
    plane = ("y", "xl", "xh")
    swap = [(0, 1), (1, 0)]
    to_right = [(i, (i + 1) % BLOCKS) for i in range(BLOCKS)]
    to_left = [((i + 1) % BLOCKS, i) for i in range(BLOCKS)]
    own = fields.reshape(T, PX, C)
    cot = cotangent.reshape(T, PX, C)
    prev = lax.ppermute(own, around, to_right)
    nxt = lax.ppermute(own, around, to_left)
    table = jnp.concatenate([neighbours.T, rotation.T, tile_owner[None]])
    vector = jnp.concatenate(
        [jnp.pad(x, (0, 64)) for x in (layer_norm_gain, layer_norm_bias)] + [up_bias]
    )
    where, wide, near_cot, up, down_t, taps, gain, bias, up_bias = run_prepare(
        table, vector[None], own, cot, up_weight, down_weight.T, depth_kernel
    )
    updated, dmix, send, keep = run_forward(
        where, prev, nxt, wide, near_cot, up, down_t, taps, gain, bias, up_bias
    )
    mine = (keep + lax.ppermute(send, "c", swap).astype(F32)).astype(BF16)
    dmix, mine = lax.optimization_barrier((dmix, mine))
    mine = lax.all_to_all(mine.reshape(16, HALF // 16, 128), plane, 0, 0)
    dpad = run_spread(dmix, taps)
    dpad, mine = lax.optimization_barrier((dpad, mine))
    mine = total_of(mine).astype(BF16)
    dpad, mine = lax.optimization_barrier((dpad, mine))
    mine = shared_with(mine, "z", 8)
    part, to_prev, to_next = run_return(where, dpad, near_cot)
    mine, to_prev, to_next = lax.optimization_barrier((mine, to_prev, to_next))
    from_right = lax.ppermute(to_prev, around, to_left)
    from_left = lax.ppermute(to_next, around, to_right)
    mine = total_of(mine).astype(BF16)
    mine = shared_with(mine, plane, 16)
    grad_fields = (part + from_right.astype(F32) + from_left.astype(F32)).astype(BF16)
    mine, grad_fields = lax.optimization_barrier((mine, grad_fields))
    mine = mine.reshape(HALF, 128)
    other = lax.ppermute(mine, "c", swap)
    core = lax.axis_index("c").astype(jnp.int32).reshape(1)
    grad_up, grad_down_t, grad_kernel, grad_gain, grad_bias, grad_up_bias = run_finish(
        core, mine, other
    )
    return (
        updated.reshape(fields.shape),
        grad_fields.reshape(fields.shape),
        grad_kernel,
        grad_gain,
        grad_bias,
        grad_up,
        grad_up_bias,
        grad_down_t.T,
    )


def solution(mesh):
    fine = Mesh(mesh.devices.reshape(4, 2, 2, 8, 2), ("y", "xl", "xh", "z", "c"))
    tiles = P(("y", "xl"), ("xh", "z", "c"), None, None, None)
    return jax.shard_map(
        on_device,
        mesh=fine,
        in_specs=(tiles, P(), P(), P(), P(), P(), P(), tiles, P(), P(), P()),
        out_specs=(tiles, tiles, P(), P(), P(), P(), P(), P()),
        check_vma=False,
    )
```

```python
import math

import jax
import jax.numpy as jnp
from jax import lax
from jax.experimental import pallas as pl
from jax.experimental.pallas import tpu as pltpu
from jax.sharding import Mesh, PartitionSpec as P

GELU_C = math.sqrt(2.0 / math.pi)
EPSILON = 1e-06
F32 = jnp.float32
BF16 = jnp.bfloat16
T = 4
S = 16
PX = S * S
C = 192
HID = 768
W = 24
DW = 32
WEIGHT_ROWS = 2 * C * HID // 128
ROWS = 2560
HALF = ROWS // 2
MIB = 1024 * 1024
SLABS = 3 * T // 2
BLOCKS = 32


def gelu_pair(value):
    square = value * value
    half = 0.5 + 0.5 * jnp.tanh(value * (GELU_C + GELU_C * 0.044715 * square))
    result = value * half
    slope = half + result * (1.0 - half) * (2.0 * GELU_C + GELU_C * 6.0 * 0.044715 * square)
    return (result, slope)


def turn_of(quarter):
    on_i = jnp.where(quarter == 0, S, jnp.where(quarter == 1, -1, jnp.where(quarter == 2, -S, 1)))
    on_j = jnp.where(quarter == 0, 1, jnp.where(quarter == 1, S, jnp.where(quarter == 2, -1, -S)))
    base = jnp.where(
        quarter == 0, 0, jnp.where(quarter == 1, S - 1, jnp.where(quarter == 2, PX - 1, PX - S))
    )
    return on_i, on_j, base


SLOTS = (
    (0, S - 3, -3, 3, 19),
    (2, 0, -3, 3, 19),
    (1, 0, S - 3, 0, 3),
    (1, 0, -19, 19, 22),
    (0, S - 3, S - 3, 0, 3),
    (0, S - 3, -19, 19, 22),
    (2, 0, S - 3, 0, 3),
    (2, 0, -19, 19, 22),
)
FIRST = (0, 3, 19)
COUNT = (3, S, 3)


def slot_match(slot, quarter, transposed):
    group, row0, col0, low, high = SLOTS[slot]
    length = COUNT[group] * W
    shape = (PX, length) if transposed else (length, PX)
    along = 1 if transposed else 0
    line = (1, length) if transposed else (length, 1)
    place = lax.broadcasted_iota(jnp.int32, line, along)
    row = place // W
    col = place - row * W
    on_i, on_j, base = turn_of(quarter)
    source = on_i * (row + row0) + on_j * (col + col0) + base
    source = jnp.where((col >= low) & (col < high), source, -1)
    return (lax.broadcasted_iota(jnp.int32, shape, 1 - along) == source).astype(F32).astype(BF16)


def block_places(block):
    place = lax.broadcasted_iota(jnp.int32, (8 * S, 1), 0)
    row = place // 8
    return row, place - row * 8 + 8 * block


def matches(source):
    at = lax.broadcasted_iota(jnp.int32, (8 * S, PX), 1)
    return (at == source).astype(F32).astype(BF16)


def centre_match(block):
    row, col = block_places(block)
    return matches(jnp.where((col >= 3) & (col < S + 3), row * S + col - 3, -1))


def side_match(slot, quarter):
    _, row0, col0, low, high = SLOTS[slot]
    row, col = block_places(0 if slot == 2 else 2)
    on_i, on_j, base = turn_of(quarter)
    source = on_i * (row + row0) + on_j * (col + col0) + base
    return matches(jnp.where((col >= low) & (col < high), source, -1))


def lane_is_low():
    return lax.broadcasted_iota(jnp.int32, (1, 128), 1) < 64


def packed_slabs(x):
    first = x[:, :128]
    rest = jnp.concatenate([x[:, 128:], jnp.zeros((x.shape[0], 64), x.dtype)], axis=1)
    crossed = pltpu.roll(first, 64, 1)
    low = lane_is_low()
    return first, jnp.where(low, rest, crossed), jnp.where(low, crossed, pltpu.roll(rest, 64, 1))


def prepare_kernel(
    table_ref,
    vector_ref,
    own_hbm,
    cot_hbm,
    up_hbm,
    down_hbm,
    kernel_hbm,
    where_ref,
    own_ref,
    cot_ref,
    up_ref,
    down_ref,
    kern,
    gain_ref,
    bias_ref,
    up_bias_ref,
    ids,
    own_raw,
    kernel_ref,
    sems,
):
    copies = [
        pltpu.make_async_copy(a, b, sems.at[k])
        for k, (a, b) in enumerate(
            (
                (kernel_hbm, kernel_ref),
                (own_hbm, own_raw),
                (up_hbm, up_ref),
                (cot_hbm, cot_ref),
                (down_hbm, down_ref),
            )
        )
    ]
    for copy in copies:
        copy.start()

    position = (lax.axis_index("xh") * 8 + lax.axis_index("z")) * 2 + lax.axis_index("c")
    first = position * T

    @pl.loop(0, 128, unroll=8)
    def _(q):
        at = table_ref[16, q] - first

        @pl.when((at >= 0) & (at < T))
        def _():
            ids[at] = q

    for tile in range(T):
        for slot in range(8):
            row = table_ref[16, table_ref[slot, ids[tile]]]
            where_ref[tile * 8 + slot] = (row - first + T) & (BLOCKS * T - 1)
            where_ref[T * 8 + tile * 8 + slot] = table_ref[8 + slot, ids[tile]]

    own_ref[:, :, C:] = jnp.zeros((T, PX, 256 - C), BF16)
    for part, value in enumerate(packed_slabs(vector_ref[:, :C])):
        gain_ref[part] = value
    for part, value in enumerate(packed_slabs(vector_ref[:, 256 : 256 + C])):
        bias_ref[part] = value
    up_bias_ref[...] = vector_ref[:, 512:]
    copies[0].wait()
    for a in range(7):
        for part, value in enumerate(packed_slabs(kernel_ref[a])):
            kern[part, 8 * a : 8 * a + 7, :] = value
    copies[1].wait()
    own_ref[:, :, :C] = own_raw[...]
    for copy in copies[2:]:
        copy.wait()


def run_prepare(*args):
    vmem = pl.BlockSpec(memory_space=pltpu.VMEM)
    smem = pl.BlockSpec(memory_space=pltpu.SMEM)
    return pl.pallas_call(
        prepare_kernel,
        out_shape=(
            jax.ShapeDtypeStruct((T * 16,), jnp.int32),
            jax.ShapeDtypeStruct((T, PX, 256), BF16),
            jax.ShapeDtypeStruct((T, PX, C), BF16),
            jax.ShapeDtypeStruct((C, HID), BF16),
            jax.ShapeDtypeStruct((C, HID), BF16),
            jax.ShapeDtypeStruct((3, 56, 128), F32),
            jax.ShapeDtypeStruct((3, 1, 128), F32),
            jax.ShapeDtypeStruct((3, 1, 128), F32),
            jax.ShapeDtypeStruct((1, HID), F32),
        ),
        in_specs=[smem, vmem] + [pl.BlockSpec(memory_space=pl.ANY)] * 5,
        out_specs=(smem,) + (vmem,) * 8,
        scratch_shapes=[
            pltpu.SMEM((T,), jnp.int32),
            pltpu.VMEM((T, PX, C), BF16),
            pltpu.VMEM((7, 7, C), F32),
            pltpu.SemaphoreType.DMA((5,)),
        ],
        compiler_params=pltpu.CompilerParams(vmem_limit_bytes=52736 * 1024),
        cost_estimate=pl.CostEstimate(flops=10**8, bytes_accessed=6 * 10**6, transcendentals=0),
    )(*args)


def repeat_taps(taps_ref, kern):
    for part in range(3):
        for a in range(7):
            for b in range(7):
                at = 8 * (a * 7 + b)
                tap = taps_ref[part, 8 * a + b : 8 * a + b + 1, :]
                kern[part, at : at + 8, :] = jnp.broadcast_to(tap, (8, 128))


def forward_kernel(
    where_ref,
    prev_ref,
    next_ref,
    own_ref,
    cot_ref,
    up_raw,
    down_ref,
    taps_ref,
    gain_ref,
    bias_ref,
    up_bias_ref,
    updated_hbm,
    dmix,
    send_ref,
    keep_ref,
    out_ref,
    src,
    pad,
    mix,
    xhat,
    inv,
    normed,
    g_up_bias,
    g_small,
    grads_ref,
    up_ref32,
    back_ref32,
    act_ref,
    d_up_ref,
    up_ref,
    kern,
    sem,
):
    low_half = lane_is_low()
    core = lax.axis_index("c")
    src[0:T, :, C:] = jnp.zeros((T, PX, 256 - C), BF16)
    src[2 * T :, :, C:] = jnp.zeros((T, PX, 256 - C), BF16)
    src[0:T, :, :C] = prev_ref[...]
    src[T : 2 * T] = own_ref[...]
    up_ref[0, :C, :] = up_raw[...]
    up_ref[0, C:, :] = jnp.zeros((64, HID), BF16)
    up_ref[1, :64, :] = jnp.zeros((64, HID), BF16)
    up_ref[1, 64:, :] = up_raw[...]
    repeat_taps(taps_ref, kern)
    src[2 * T :, :, :C] = next_ref[...]
    g_up_bias[...] = jnp.zeros_like(g_up_bias)
    g_small[...] = jnp.zeros_like(g_small)
    dmix[...] = jnp.zeros_like(dmix)
    grads_ref[...] = jnp.zeros_like(grads_ref)
    def put_rows(pair, half, start, count, value):
        rows = pl.ds(start, count)
        if half == 0:
            pad[pair * 3, rows, :] = value[:, :128]
            pad[pair * 3 + 1, rows, :] = value[:, 128:]
        else:
            pad[pair * 3 + 1, rows, :] += value[:, :128]
            pad[pair * 3 + 2, rows, :] = value[:, 128:]

    def put(pair, half, start, count, value):
        put_rows(pair, half, start, count, value if half == 0 else pltpu.roll(value, 64, 1))

    @pl.loop(0, T // 2)
    def _(pair):
        for half in range(2):
            tile = pair * 2 + half
            for group in (0, 2):
                total = None
                for slot in range(8):
                    if SLOTS[slot][0] != group:
                        continue
                    match = slot_match(slot, where_ref[T * 8 + tile * 8 + slot], False)
                    piece = jnp.dot(
                        match, src[where_ref[tile * 8 + slot]], preferred_element_type=F32
                    )
                    total = piece if total is None else total + piece
                put(pair, half, FIRST[group] * W, COUNT[group] * W, total)
            for block in range(3):
                total = jnp.dot(centre_match(block), src[T + tile], preferred_element_type=F32)
                if block != 1:
                    slot = 2 + block // 2
                    match = side_match(slot, where_ref[T * 8 + tile * 8 + slot])
                    total += jnp.dot(
                        match, src[where_ref[tile * 8 + slot]], preferred_element_type=F32
                    )
                if half == 1:
                    total = pltpu.roll(total, 64, 1)
                for i in range(S):
                    put_rows(pair, half, (i + 3) * W + 8 * block, 8, total[8 * i : 8 * i + 8])

    @pl.loop(0, 3 * T // 2)
    def _(slab):
        part = lax.rem(slab, 3)
        for half in range(2):
            for b in range(7):
                acc = [None] * S
                taps = [kern[part, pl.ds(8 * (a * 7 + b), 8), :] for a in range(7)]
                for m in range(S + 6):
                    x = pad[slab, pl.ds(m * W + b + 8 * half, 8), :]
                    for a in range(7):
                        i = m - a
                        if 0 <= i < S:
                            term = x * taps[a]
                            acc[i] = term if acc[i] is None else acc[i] + term
                for i in range(S):
                    rows = pl.ds(i * S + 8 * half, 8)
                    mix[slab, rows, :] = acc[i] if b == 0 else mix[slab, rows, :] + acc[i]

    def pair_means(s0, s1, s2):
        first = jnp.sum(s0 + jnp.where(low_half, s1, 0.0), axis=1, keepdims=True) * (1.0 / C)
        second = jnp.sum(s2 + jnp.where(low_half, 0.0, s1), axis=1, keepdims=True) * (1.0 / C)
        return first, jnp.where(low_half, first, second), second

    CH = 64

    @pl.loop(0, (T // 2) * (PX // CH), unroll=8)
    def _(step):
        pair = step // (PX // CH)
        rows = pl.ds(pl.multiple_of(lax.rem(step, PX // CH) * CH, CH), CH)
        slabs = [mix[pair * 3 + k, rows, :] for k in range(3)]
        means = pair_means(*slabs)
        slabs = [x - m for x, m in zip(slabs, means)]
        spreads = pair_means(*[x * x for x in slabs])
        for k in range(3):
            deviation = jnp.broadcast_to(lax.rsqrt(spreads[k] + EPSILON), (CH, 128))
            standard = slabs[k] * deviation
            inv[pair * 3 + k, rows, :] = deviation
            xhat[pair * 3 + k, rows, :] = standard
            normed[pair, rows, 128 * k : 128 * (k + 1)] = (
                standard * gain_ref[k] + bias_ref[k]
            ).astype(BF16)

    def enter(step, half, chunk, x, cot):
        hid = slice(256 * chunk, 256 * (chunk + 1))
        up_ref32[step % 3] = jnp.dot(x, up_ref[half, :, hid], preferred_element_type=F32)
        back_ref32[step % 3] = jnp.dot(cot, down_ref[:, hid], preferred_element_type=F32)

    @pl.loop(0, T // 2, unroll=2)
    def _(pair):
        xs = [normed[pair, :, 128 * half : 128 * half + 256] for half in range(2)]
        cots = [cot_ref[pair * 2 + half] for half in range(2)]
        steps = [(half, chunk) for half in range(2) for chunk in range(3)]
        enter(0, 0, 0, xs[0], cots[0])
        for step, (half, chunk) in enumerate(steps):
            if step + 1 < len(steps):
                after = steps[step + 1]
                enter(step + 1, *after, xs[after[0]], cots[after[0]])
            hid = slice(256 * chunk, 256 * (chunk + 1))
            if chunk == 0:
                x_t = jnp.transpose(xs[half].astype(F32)).astype(BF16)
                cot_t = jnp.transpose(cots[half].astype(F32)).astype(BF16)
                branch = jnp.zeros((PX, C), F32)
                normed_grad = jnp.zeros((PX, 256), F32)
            slot = step % 3
            bias_sum = jnp.zeros((8, 256), F32)
            for r in range(0, PX, 16):
                rows = slice(r, r + 16)
                value, slope = gelu_pair(up_ref32[slot, rows, :] + up_bias_ref[:, hid])
                d_up = back_ref32[slot, rows, :] * slope
                bias_sum += d_up[:8] + d_up[8:]
                act_ref[slot, rows, :] = value.astype(BF16)
                d_up_ref[slot, rows, :] = d_up.astype(BF16)
            g_up_bias[:, hid] += bias_sum
            activation = act_ref[slot]
            d_up_b = d_up_ref[slot]
            branch += times_transposed(activation, down_ref[:, hid])
            down_grad = jnp.dot(cot_t, activation, preferred_element_type=F32)
            up_grad = jnp.dot(x_t, d_up_b, preferred_element_type=F32)
            for k in range(2):
                at = C * (2 * chunk + k)
                lanes = slice(128 * k, 128 * (k + 1))
                grads_ref[at : at + C, :] += up_grad[64 * half : 64 * half + C, lanes]
                at += WEIGHT_ROWS // 2
                grads_ref[at : at + C, :] += down_grad[:, lanes]
            normed_grad += times_transposed(d_up_b, up_ref[half, :, hid])
            if chunk == 2:
                tile = pair * 2 + half
                own = src[T + tile, :, :C].astype(F32)
                out_ref[tile] = (own + branch).astype(BF16)
                if half == 0:
                    mix[pair * 3] = normed_grad[:, :128]
                    mix[pair * 3 + 1] = normed_grad[:, 128:]
                else:
                    mix[pair * 3 + 1] += normed_grad[:, :128]
                    mix[pair * 3 + 2] = normed_grad[:, 128:]

    @pl.loop(0, (T // 2) * (PX // CH), unroll=8)
    def _(step):
        pair = step // (PX // CH)
        start = pl.multiple_of(lax.rem(step, PX // CH) * CH, CH)
        rows = pl.ds(start, CH)
        grads = [mix[pair * 3 + k, rows, :] for k in range(3)]
        standard = [xhat[pair * 3 + k, rows, :] for k in range(3)]
        for k in range(3):
            g_small[k, 8 * 49 : 8 * 50, :] += jnp.sum(
                (grads[k] * standard[k]).reshape(CH // 8, 8, 128), axis=0
            )
            g_small[k, 8 * 50 : 8 * 51, :] += jnp.sum(grads[k].reshape(CH // 8, 8, 128), axis=0)
        scaled = [grads[k] * gain_ref[k] for k in range(3)]
        means = pair_means(*scaled)
        products = pair_means(*[e * x for e, x in zip(scaled, standard)])
        for k in range(3):
            d_mixed = inv[pair * 3 + k, rows, :] * (
                scaled[k] - means[k] - standard[k] * products[k]
            )
            for r in range(CH // S):
                at = (start // S + r) * DW + 8
                dmix[pair * 3 + k, pl.ds(pl.multiple_of(at, 8), S), :] = d_mixed[r * S : (r + 1) * S]

    result = pltpu.make_async_copy(out_ref, updated_hbm, sem)
    result.start()

    @pl.loop(0, 3 * T // 2)
    def _(slab):
        part = lax.rem(slab, 3)
        for half in range(2):
            grads = [dmix[slab, pl.ds(i * DW + 8 + 8 * half, 8), :] for i in range(S)]
            for b in range(7):
                acc = [None] * 7
                for m in range(S + 6):
                    x = pad[slab, pl.ds(m * W + b + 8 * half, 8), :]
                    for a in range(7):
                        i = m - a
                        if 0 <= i < S:
                            term = x * grads[i]
                            acc[a] = term if acc[a] is None else acc[a] + term
                for a in range(7):
                    g_small[part, 8 * (a * 7 + b) : 8 * (a * 7 + b + 1), :] += acc[a]
    sums = [jnp.sum(g_small[k].reshape(56, 8, 128), axis=1) for k in range(3)]
    crossed = pltpu.roll(jnp.where(low_half, sums[2], sums[1]), 64, 1)
    grads_ref[WEIGHT_ROWS : WEIGHT_ROWS + 56, :] = (sums[0] + crossed)
    grads_ref[WEIGHT_ROWS + 56 : WEIGHT_ROWS + 112, :] = (
        sums[1] + pltpu.roll(sums[2], 64, 1)
    )
    bias_sum = jnp.sum(g_up_bias[...], axis=0, keepdims=True)
    bias_rows = jnp.concatenate(
        [bias_sum[:, 128 * k : 128 * (k + 1)] for k in range(6)] + [jnp.zeros((10, 128), F32)],
        axis=0,
    )
    grads_ref[WEIGHT_ROWS + 112 : WEIGHT_ROWS + 128, :] = bias_rows
    send_ref[...] = grads_ref[pl.ds((1 - core) * HALF, HALF), :].astype(BF16)
    keep_ref[...] = grads_ref[pl.ds(core * HALF, HALF), :]
    result.wait()


def times_transposed(x, y):
    return lax.dot_general(x, y, (((1,), (1,)), ((), ())), preferred_element_type=F32)


def run_forward(*args):
    vmem = pl.BlockSpec(memory_space=pltpu.VMEM)
    smem = pl.BlockSpec(memory_space=pltpu.SMEM)
    slab = pltpu.VMEM((SLABS, PX, 128), F32)
    return pl.pallas_call(
        forward_kernel,
        out_shape=(
            jax.ShapeDtypeStruct((T, PX, C), BF16),
            jax.ShapeDtypeStruct((SLABS, S * DW, 128), F32),
            jax.ShapeDtypeStruct((HALF, 128), BF16),
            jax.ShapeDtypeStruct((HALF, 128), F32),
        ),
        in_specs=[smem] + [vmem] * 10,
        out_specs=(pl.BlockSpec(memory_space=pl.ANY), vmem, vmem, vmem),
        scratch_shapes=[
            pltpu.VMEM((T, PX, C), BF16),
            pltpu.VMEM((3 * T, PX, 256), BF16),
            pltpu.VMEM((SLABS, 22 * W, 128), F32),
            slab,
            slab,
            slab,
            pltpu.VMEM((T // 2, PX, 384), BF16),
            pltpu.VMEM((8, HID), F32),
            pltpu.VMEM((3, 8 * 56, 128), F32),
            pltpu.VMEM((ROWS, 128), F32),
            pltpu.VMEM((3, PX, 256), F32),
            pltpu.VMEM((3, PX, 256), F32),
            pltpu.VMEM((3, PX, 256), BF16),
            pltpu.VMEM((3, PX, 256), BF16),
            pltpu.VMEM((2, 256, HID), BF16),
            pltpu.VMEM((3, 8 * 49, 128), F32),
            pltpu.SemaphoreType.DMA,
        ],
        compiler_params=pltpu.CompilerParams(vmem_limit_bytes=24 * MIB),
        cost_estimate=pl.CostEstimate(flops=4 * 10**9, bytes_accessed=8 * 10**6, transcendentals=10**6),
    )(*args)


def spread_kernel(dmix, taps_ref, dpad, kern):
    repeat_taps(taps_ref, kern)

    @pl.loop(0, SLABS)
    def _(slab):
        part = lax.rem(slab, 3)
        for third in range(3):
            for b in range(7):
                acc = [None] * (S + 6)
                taps = [kern[part, pl.ds(8 * (a * 7 + b), 8), :] for a in range(7)]
                for i in range(S):
                    x = dmix[slab, pl.ds(i * DW + 8 + 8 * third - b, 8), :]
                    for a in range(7):
                        term = x * taps[a]
                        acc[i + a] = term if acc[i + a] is None else acc[i + a] + term
                for m in range(S + 6):
                    rows = pl.ds(m * W + 8 * third, 8)
                    dpad[slab, rows, :] = acc[m] if b == 0 else dpad[slab, rows, :] + acc[m]


def run_spread(dmix, taps):
    vmem = pl.BlockSpec(memory_space=pltpu.VMEM)
    return pl.pallas_call(
        spread_kernel,
        out_shape=jax.ShapeDtypeStruct((SLABS, 22 * W, 128), F32),
        in_specs=[vmem] * 2,
        out_specs=vmem,
        scratch_shapes=[pltpu.VMEM((3, 8 * 49, 128), F32)],
        compiler_params=pltpu.CompilerParams(vmem_limit_bytes=12 * MIB),
        cost_estimate=pl.CostEstimate(flops=10**9, bytes_accessed=5 * 10**6, transcendentals=0),
    )(dmix, taps)


def return_kernel(where_ref, dpad, cot_ref, part_ref, to_prev_ref, to_next_ref, collected):
    collected[...] = jnp.zeros_like(collected)

    @pl.loop(0, T // 2)
    def _(pair):
        for half in range(2):
            tile = pair * 2 + half
            for slot in range(8):
                group = SLOTS[slot][0]
                rows = pl.ds(FIRST[group] * W, COUNT[group] * W)
                border = jnp.concatenate(
                    [dpad[pair * 3 + half + k, rows, :] for k in range(2)], axis=1
                ).astype(BF16)
                match = slot_match(slot, where_ref[T * 8 + tile * 8 + slot], True)
                piece = jnp.dot(match, border, preferred_element_type=F32)
                if half == 1:
                    piece = pltpu.roll(piece, 192, 1)
                collected[where_ref[tile * 8 + slot]] += piece

    to_prev_ref[...] = collected[0:T, :, :C].astype(BF16)
    to_next_ref[...] = collected[2 * T :, :, :C].astype(BF16)

    @pl.loop(0, T // 2)
    def _(pair):
        for half in range(2):
            tile = pair * 2 + half
            for i in range(S):
                rows = slice(i * S, (i + 1) * S)
                centre = jnp.concatenate(
                    [dpad[pair * 3 + half + k, pl.ds((i + 3) * W + 3, S), :] for k in range(2)],
                    axis=1,
                )
                if half == 1:
                    centre = pltpu.roll(centre, 192, 1)
                part_ref[tile, rows, :] = (
                    cot_ref[tile, rows, :].astype(F32)
                    + centre[:, :C]
                    + collected[T + tile, rows, :C]
                )


def run_return(where, dpad, cot):
    vmem = pl.BlockSpec(memory_space=pltpu.VMEM)
    smem = pl.BlockSpec(memory_space=pltpu.SMEM)
    tile = (T, PX, C)
    return pl.pallas_call(
        return_kernel,
        out_shape=(
            jax.ShapeDtypeStruct(tile, F32),
            jax.ShapeDtypeStruct(tile, BF16),
            jax.ShapeDtypeStruct(tile, BF16),
        ),
        in_specs=[smem, vmem, vmem],
        out_specs=(vmem,) * 3,
        scratch_shapes=[pltpu.VMEM((3 * T, PX, 256), F32)],
        compiler_params=pltpu.CompilerParams(vmem_limit_bytes=16 * MIB),
        cost_estimate=pl.CostEstimate(flops=10**9, bytes_accessed=5 * 10**6, transcendentals=0),
    )(where, dpad, cot)


def finish_kernel(
    core_ref, mine_ref, other_ref, up_out, down_out, kernel_out, gain_out, bias_out, up_bias_out, halves
):
    scale = 1.0 / math.sqrt(8 * BLOCKS * T * PX)
    core = core_ref[0]
    halves[core] = mine_ref[...]
    halves[1 - core] = other_ref[...]

    def rows(start, count):
        side, at = divmod(start, HALF)
        if at + count <= HALF:
            return halves[side, at : at + count, :].astype(F32) * scale
        split = HALF - at
        return jnp.concatenate([rows(start, split), rows(start + split, count - split)], axis=0)

    for k in range(HID // 128):
        up_out[:, 128 * k : 128 * (k + 1)] = rows(C * k, C)
        down_out[:, 128 * k : 128 * (k + 1)] = rows(WEIGHT_ROWS // 2 + C * k, C)
    small = jnp.concatenate(
        [rows(WEIGHT_ROWS, 56), rows(WEIGHT_ROWS + 56, 56)[:, :64]], axis=1
    )
    for a in range(7):
        kernel_out[a] = small[7 * a : 7 * (a + 1)]
    gain_out[...] = small[49:50].reshape(C)
    bias_out[...] = small[50:51].reshape(C)
    bias = rows(WEIGHT_ROWS + 112, 16)
    for k in range(HID // 128):
        up_bias_out[128 * k : 128 * (k + 1)] = bias[k : k + 1].reshape(128)


def run_finish(core, mine, other):
    vmem = pl.BlockSpec(memory_space=pltpu.VMEM)
    smem = pl.BlockSpec(memory_space=pltpu.SMEM)
    return pl.pallas_call(
        finish_kernel,
        out_shape=(
            jax.ShapeDtypeStruct((C, HID), F32),
            jax.ShapeDtypeStruct((C, HID), F32),
            jax.ShapeDtypeStruct((7, 7, C), F32),
            jax.ShapeDtypeStruct((C,), F32),
            jax.ShapeDtypeStruct((C,), F32),
            jax.ShapeDtypeStruct((HID,), F32),
        ),
        in_specs=[smem, vmem, vmem],
        out_specs=(vmem,) * 6,
        scratch_shapes=[pltpu.VMEM((2, HALF, 128), BF16)],
        compiler_params=pltpu.CompilerParams(vmem_limit_bytes=8 * MIB),
        cost_estimate=pl.CostEstimate(flops=10**6, bytes_accessed=2 * 10**6, transcendentals=0),
    )(core, mine, other)


def shared_with(x, axes, count):
    return lax.all_to_all(jnp.broadcast_to(x[None], (count,) + x.shape), axes, 0, 0)


def total_of(x):
    return jnp.sum(x.astype(F32), axis=0)


def on_device(
    fields,
    depth_kernel,
    layer_norm_gain,
    layer_norm_bias,
    up_weight,
    up_bias,
    down_weight,
    cotangent,
    neighbours,
    rotation,
    tile_owner,
):
    around = ("xh", "z", "c")
    plane = ("y", "xl", "xh")
    swap = [(0, 1), (1, 0)]
    to_right = [(i, (i + 1) % BLOCKS) for i in range(BLOCKS)]
    to_left = [((i + 1) % BLOCKS, i) for i in range(BLOCKS)]
    own = fields.reshape(T, PX, C)
    cot = cotangent.reshape(T, PX, C)
    prev = lax.ppermute(own, around, to_right)
    nxt = lax.ppermute(own, around, to_left)
    table = jnp.concatenate([neighbours.T, rotation.T, tile_owner[None]])
    vector = jnp.concatenate(
        [jnp.pad(x, (0, 64)) for x in (layer_norm_gain, layer_norm_bias)] + [up_bias]
    )
    where, wide, near_cot, up, down_t, taps, gain, bias, up_bias = run_prepare(
        table, vector[None], own, cot, up_weight, down_weight.T, depth_kernel
    )
    updated, dmix, send, keep = run_forward(
        where, prev, nxt, wide, near_cot, up, down_t, taps, gain, bias, up_bias
    )
    mine = (keep + lax.ppermute(send, "c", swap).astype(F32)).astype(BF16)
    dmix, mine = lax.optimization_barrier((dmix, mine))
    mine = lax.all_to_all(mine.reshape(16, HALF // 16, 128), plane, 0, 0)
    dpad = run_spread(dmix, taps)
    dpad, mine = lax.optimization_barrier((dpad, mine))
    mine = total_of(mine).astype(BF16)
    dpad, mine = lax.optimization_barrier((dpad, mine))
    mine = shared_with(mine, "z", 8)
    part, to_prev, to_next = run_return(where, dpad, near_cot)
    mine, to_prev, to_next = lax.optimization_barrier((mine, to_prev, to_next))
    from_right = lax.ppermute(to_prev, around, to_left)
    from_left = lax.ppermute(to_next, around, to_right)
    mine = total_of(mine).astype(BF16)
    mine = shared_with(mine, plane, 16)
    grad_fields = (part + from_right.astype(F32) + from_left.astype(F32)).astype(BF16)
    mine, grad_fields = lax.optimization_barrier((mine, grad_fields))
    mine = mine.reshape(HALF, 128)
    other = lax.ppermute(mine, "c", swap)
    core = lax.axis_index("c").astype(jnp.int32).reshape(1)
    grad_up, grad_down_t, grad_kernel, grad_gain, grad_bias, grad_up_bias = run_finish(
        core, mine, other
    )
    return (
        updated.reshape(fields.shape),
        grad_fields.reshape(fields.shape),
        grad_kernel,
        grad_gain,
        grad_bias,
        grad_up,
        grad_up_bias,
        grad_down_t.T,
    )


def solution(mesh):
    fine = Mesh(mesh.devices.reshape(4, 2, 2, 8, 2), ("y", "xl", "xh", "z", "c"))
    tiles = P(("y", "xl"), ("xh", "z", "c"), None, None, None)
    return jax.shard_map(
        on_device,
        mesh=fine,
        in_specs=(tiles, P(), P(), P(), P(), P(), P(), tiles, P(), P(), P()),
        out_specs=(tiles, tiles, P(), P(), P(), P(), P(), P()),
        check_vma=False,
    )
```
